128 devices in a mesh: dp: 2 (over x_lo), lat: 4 (over y), lon: 16 (over x_hi, z, core).
Axes of the slice: x: 4 (x_hi: 2, x_lo: 2; x = x_hi * 2 + x_lo), y: 4, z: 4, core: 2. Of those that a mesh axis runs over, the one named last changes fastest.
Arguments:
- inputs: bfloat16 [2, 128, 256, 1024], P('dp', 'lat', 'lon'), may hold values from -40 to 40
- grad_out: bfloat16 [2, 128, 256, 1024], P('dp', 'lat', 'lon'), may hold values from -6 to 6
- w_qkv: bfloat16 [1024, 3072], replicated, may hold values from -0.1875 to 0.1875
Outputs:
- grad_inputs: bfloat16 [2, 128, 256, 1024], P('dp', 'lat', 'lon')
- grad_w_qkv: float32 [1024, 3072], P(('dp', 'lat', 'lon'))
The draws below stay inside these ranges and needn't reach their ends.
All inputs are finite; a program needn't handle non-finite values.
Results may differ from the reference program's by a relative error of at most 0.011.
Values may be sent and summed in bfloat16 or wider, within the bound.
A program may use at most 192 MiB of HBM per device.

```python
import jax
import jax.numpy as jnp
from jax import lax

D = 1024
HEADS = 16
WIN = 13
LAT_DEV = 32
LON_DEV = 16
TILE_R = 8
TILE_C = 16
GROUP = 4
SAMPLES = 2
ROWS = 128
COLS = 256
TOKENS = 65536
N_LAT = 4
N_LON = 16
DEVICES = 128


def draw_inputs(key, part):
    base_key = jax.random.fold_in(key, 11)
    noise_key, pair_key = jax.random.split(base_key, 2)
    noise_field = jnp.clip(jax.random.normal(noise_key, (SAMPLES, ROWS, COLS, D), jnp.float32), -5.0, 5.0)
    sample_ids = jnp.arange(SAMPLES, dtype=jnp.int32)[:, None, None]
    band_ids = (jnp.arange(ROWS, dtype=jnp.int32) // LAT_DEV)[None, :, None]
    column_ids = (jnp.arange(COLS, dtype=jnp.int32) // LON_DEV)[None, None, :]
    owner_ids = (sample_ids * N_LAT + band_ids) * N_LON + column_ids
    pairing = jax.random.permutation(pair_key, DEVICES).astype(jnp.int32)
    target = pairing[owner_ids]
    feature_block = jnp.arange(D, dtype=jnp.int32) // (D // DEVICES)
    factor = jnp.where(target[..., None] == feature_block, 4.0, 1.0)
    values = noise_field * factor
    return values.astype(jnp.bfloat16)


def level_of(key, extent, cuts, least, high):
    gain, own = 1.0, jax.random.fold_in(key, 6)
    for position, blocks in cuts:
        heights = jnp.exp(jax.random.uniform(jax.random.fold_in(own, position), (blocks,), jnp.float32, least / len(cuts), high / len(cuts)))
        gain = gain * jnp.repeat(heights, extent[position] // blocks).reshape([-1 if axis == position else 1 for axis in range(len(extent))])
    return gain


def noise(key, dims, deviation, limit, cuts=(), held_as=jnp.bfloat16):
    entries = deviation * jax.random.normal(key, dims, jnp.float32)
    if cuts:
        entries = entries * level_of(key, dims, cuts, -0.22, 0.18)
    return jnp.clip(entries, -limit, limit).astype(held_as)


def setup_inputs(seed: int = 0) -> dict:
    seeds = jax.random.split(jax.random.key(seed), 4)
    inputs = draw_inputs(jax.random.fold_in(seeds[3], 71), 0)
    grad_out = noise(seeds[1], (SAMPLES, ROWS, COLS, D), 1.0, 6.0, ((0, 2), (1, 4), (2, 16)))
    w_qkv = noise(seeds[2], (D, 3 * D), D ** -0.5, 0.1875)
    return dict(inputs=inputs, grad_out=grad_out, w_qkv=w_qkv)


def tile_layout(row_tile, band_start, band_rows, total_rows):
    margin = WIN // 2
    first_row = band_start + row_tile * TILE_R
    window_top = jnp.clip(first_row - margin, 0, total_rows - WIN)
    region_top = jnp.minimum(window_top - band_start + margin, band_rows - TILE_R)
    query_rows = first_row + jnp.arange(TILE_R, dtype=jnp.int32)
    key_rows = region_top + band_start - margin + jnp.arange(TILE_R + WIN - 1, dtype=jnp.int32)
    return region_top, query_rows, key_rows


def window_mask(query_rows, key_rows, total_rows):
    margin = WIN // 2
    starts = jnp.clip(query_rows - margin, 0, total_rows - WIN)
    row_inside = (key_rows[:, None] >= starts[None, :]) & (key_rows[:, None] <= starts[None, :] + WIN - 1)
    query_cols = jnp.arange(TILE_C, dtype=jnp.int32)
    key_cols = jnp.arange(TILE_C + WIN - 1, dtype=jnp.int32)
    col_inside = (key_cols[:, None] >= query_cols[None, :]) & (key_cols[:, None] <= query_cols[None, :] + WIN - 1)
    inside = row_inside[:, None, :, None] & col_inside[None, :, None, :]
    return inside.reshape((TILE_R + WIN - 1) * (TILE_C + WIN - 1), TILE_R * TILE_C)


def rounded(tensor):
    narrow = lax.optimization_barrier(tensor.astype(jnp.bfloat16))
    return narrow.astype(jnp.float32)


def tile_grads(query_tile, grad_tile, region, inside):
    query_count, width = query_tile.shape
    key_count = region.shape[0]
    head_width = width // HEADS
    norm_scale = head_width ** -0.5
    head_queries = query_tile.astype(jnp.float32).reshape(query_count, HEADS, head_width)
    head_grads = grad_tile.astype(jnp.float32).reshape(query_count, HEADS, head_width)
    head_keys = region[:, :width].astype(jnp.float32).reshape(key_count, HEADS, head_width)
    head_values = region[:, width:].astype(jnp.float32).reshape(key_count, HEADS, head_width)
    scores = jnp.einsum('khd,ihd->hki', head_keys, head_queries) * norm_scale
    scores = jnp.where(inside[None], scores, -1e30)
    maxima = jnp.max(scores, axis=1, keepdims=True)
    exponent = jnp.exp(scores - maxima)
    attn_weights = exponent / jnp.sum(exponent, axis=1, keepdims=True)
    attn_rounded = rounded(attn_weights)
    value_dots = jnp.einsum('khd,ihd->hki', head_values, head_grads)
    delta_terms = jnp.sum(attn_weights * value_dots, axis=1, keepdims=True)
    score_grads = rounded(attn_weights * (value_dots - delta_terms))
    query_grad = jnp.einsum('hki,khd->ihd', score_grads, head_keys) * norm_scale
    key_grad = jnp.einsum('hki,ihd->khd', score_grads, head_queries) * norm_scale
    value_grad = jnp.einsum('hki,ihd->khd', attn_rounded, head_grads)
    region_grad = jnp.concatenate([key_grad.reshape(key_count, width), value_grad.reshape(key_count, width)], axis=1)
    return query_grad.reshape(query_count, width), region_grad


def run_tiles(queries, grad_out, key_values, band_start, total_rows):
    samples, band_rows, band_cols, width = queries.shape
    region_rows = TILE_R + WIN - 1
    region_cols = TILE_C + WIN - 1
    row_tiles = band_rows // TILE_R
    col_tiles = band_cols // TILE_C
    tile_count = samples * row_tiles * col_tiles
    anchor = jnp.zeros((), jnp.int32)

    def one_tile(tile_index):
        sample = tile_index // (row_tiles * col_tiles)
        row_tile = (tile_index // col_tiles) % row_tiles
        col_tile = tile_index % col_tiles
        region_top, query_rows, key_rows = tile_layout(row_tile, band_start, band_rows, total_rows)
        first_col = col_tile * TILE_C
        query_tile = lax.dynamic_slice(queries, (sample, row_tile * TILE_R, first_col, anchor), (1, TILE_R, TILE_C, width)).reshape(TILE_R * TILE_C, width)
        grad_tile = lax.dynamic_slice(grad_out, (sample, row_tile * TILE_R, first_col, anchor), (1, TILE_R, TILE_C, width)).reshape(TILE_R * TILE_C, width)
        region = lax.dynamic_slice(key_values, (sample, region_top, first_col, anchor), (1, region_rows, region_cols, 2 * width)).reshape(region_rows * region_cols, 2 * width)
        query_grad, region_grad = tile_grads(query_tile, grad_tile, region, window_mask(query_rows, key_rows, total_rows))
        return query_grad, region_grad, sample, region_top, first_col

    def group_step(totals, group_index):
        tile_ids = group_index * GROUP + jnp.arange(GROUP, dtype=jnp.int32)
        query_grads, region_grads, sample_ids, region_tops, region_lefts = jax.vmap(one_tile)(tile_ids)
        for member in range(GROUP):
            corner = (sample_ids[member], region_tops[member], region_lefts[member], anchor)
            current = lax.dynamic_slice(totals, corner, (1, region_rows, region_cols, 2 * width))
            totals = lax.dynamic_update_slice(totals, current + region_grads[member].reshape(1, region_rows, region_cols, 2 * width), corner)
        return totals, query_grads

    initial = jnp.zeros((samples, band_rows + WIN - 1, band_cols + WIN - 1, 2 * width), jnp.float32)
    totals, query_grads = lax.scan(group_step, initial, jnp.arange(tile_count // GROUP, dtype=jnp.int32))
    query_grads = query_grads.reshape(samples, row_tiles, col_tiles, TILE_R, TILE_C, width)
    query_grads = query_grads.transpose(0, 1, 3, 2, 4, 5).reshape(samples, band_rows, band_cols, width)
    return query_grads, totals


def reference(inputs, grad_out, w_qkv):
    samples, total_rows, total_cols, width = inputs.shape
    margin = WIN // 2
    flat_inputs = inputs.reshape(-1, width)
    projected = jnp.dot(flat_inputs, w_qkv, preferred_element_type=jnp.float32).astype(jnp.bfloat16)
    projected = projected.reshape(samples, total_rows, total_cols, 3 * width)
    queries = projected[..., :width]
    key_values = projected[..., width:]
    key_values = jnp.concatenate([key_values[:, :, total_cols - margin:], key_values, key_values[:, :, :margin]], axis=2)
    zero_rows = jnp.zeros((samples, margin, total_cols + 2 * margin, 2 * width), key_values.dtype)
    key_values = jnp.concatenate([zero_rows, key_values, zero_rows], axis=1)
    band_start = jnp.zeros((), jnp.int32)
    query_grads, totals = run_tiles(queries, grad_out, key_values, band_start, total_rows)
    totals = totals[:, margin:total_rows + margin]
    interior = totals[:, :, margin:total_cols + margin]
    interior = interior.at[:, :, :margin].add(totals[:, :, total_cols + margin:])
    interior = interior.at[:, :, total_cols - margin:].add(totals[:, :, :margin])
    grad_proj = jnp.concatenate([query_grads.astype(jnp.bfloat16), interior.astype(jnp.bfloat16)], axis=-1).reshape(-1, 3 * width)
    grad_inputs = jnp.dot(grad_proj, w_qkv.T, preferred_element_type=jnp.float32).astype(jnp.bfloat16)
    grad_inputs = grad_inputs.reshape(inputs.shape)
    grad_w_qkv = jnp.dot(flat_inputs.T, grad_proj, preferred_element_type=jnp.float32) * (float(TOKENS) ** -0.5)
    return grad_inputs, grad_w_qkv
```

```python
import functools

import jax
import jax.numpy as jnp
from jax import lax
from jax.experimental import pallas as pl
from jax.experimental.pallas import tpu as pltpu
from jax.sharding import PartitionSpec as P

WIN = 13
MARGIN = WIN // 2
HEAD = 64
QUAD = 4
WIDTH = QUAD * HEAD
LAT_DEV = 32
LON_DEV = 16
ROW_T = 4
TILES = LAT_DEV // ROW_T
QUERIES = ROW_T * LON_DEV
KEY_ROWS = ROW_T + WIN - 1
SIDE = 2 * MARGIN
KEYS_A = KEY_ROWS * LON_DEV
KEYS_B = KEY_ROWS * SIDE
KEYS = KEYS_A + KEYS_B
PAD_ROWS = 2
OWN = (PAD_ROWS + MARGIN) * LON_DEV
OWN_N = LAT_DEV * LON_DEV
SPLIT = (PAD_ROWS + LAT_DEV + SIDE) * LON_DEV
TOKENS = 1280
D = 1024
NT = (((1,), (1,)), ((), ()))
TN = (((0,), (0,)), ((), ()))
NN = (((1,), (0,)), ((), ()))
MESH = pl.DeviceIdType.MESH


def mm(a, b, dims=NN):
    return lax.dot_general(a, b, dims, preferred_element_type=jnp.float32)


def key_tile(t, first_band, last_band):
    lead = jnp.logical_and(first_band, t == 0).astype(jnp.int32)
    tail = jnp.logical_and(last_band, t == TILES - 1).astype(jnp.int32)
    return t + lead - tail


def window_bias(t, top, keys, side, band_start, total_rows):
    kk = lax.broadcasted_iota(jnp.int32, (keys, WIDTH), 0)
    qq = lax.broadcasted_iota(jnp.int32, (keys, WIDTH), 1) & (QUERIES - 1)
    i, j = qq >> 4, qq & 15
    if side:
        r = (kk * 171) >> 11
        c = kk - r * SIDE
        col = jnp.where(c < MARGIN, c - MARGIN, c + (LON_DEV - MARGIN))
    else:
        r, col = kk >> 4, kk & 15
    first = band_start + ROW_T * t
    key_row = band_start + ROW_T * top - MARGIN + r
    start = jnp.clip(first + i - MARGIN, 0, total_rows - WIN)
    off = key_row - start
    away = col - j
    inside = (off >= 0) & (off < WIN) & (away >= -MARGIN) & (away <= MARGIN)
    return jnp.where(inside, 0.0, -1e30).astype(jnp.float32)


def spread(tile, same_head):
    return jnp.concatenate([tile] * QUAD, axis=0) * same_head


def attend(t, top, q, k, v, go, bias, same, dk, dv, dq):
    own = pl.ds(t * QUERIES, QUERIES)
    ka = pl.ds(pl.multiple_of(PAD_ROWS * LON_DEV + top * QUERIES, 32), KEYS_A)
    kb = pl.ds(pl.multiple_of(SPLIT + top * ROW_T * SIDE, 16), KEYS_B)
    same_head = same[...]
    bq = spread(q[own, :], same_head)
    bg = spread(go[own, :], same_head)
    sa = mm(k[ka, :], bq, NT) + bias[t, :KEYS_A, :]
    sb = mm(k[kb, :], bq, NT) + bias[t, KEYS_A:, :]
    peak = jnp.maximum(jnp.max(sa, axis=0, keepdims=True), jnp.max(sb, axis=0, keepdims=True))
    pa = jnp.exp(sa - peak)
    pb = jnp.exp(sb - peak)
    da = mm(v[ka, :], bg, NT)
    db = mm(v[kb, :], bg, NT)
    inv = 1.0 / (jnp.sum(pa, axis=0, keepdims=True) + jnp.sum(pb, axis=0, keepdims=True))
    delta = (
        jnp.sum(pa * da, axis=0, keepdims=True) + jnp.sum(pb * db, axis=0, keepdims=True)
    ) * inv
    pa = pa * inv
    pb = pb * inv
    aa = pa.astype(jnp.bfloat16)
    ab = pb.astype(jnp.bfloat16)
    ea = (pa * (da - delta)).astype(jnp.bfloat16)
    eb = (pb * (db - delta)).astype(jnp.bfloat16)
    dk[ka, :] += mm(ea, bq)
    dk[kb, :] += mm(eb, bq)
    dv[ka, :] += mm(aa, bg)
    dv[kb, :] += mm(ab, bg)
    mixed = (mm(ea, k[ka, :], TN) + mm(eb, k[kb, :], TN)) * same_head.astype(jnp.float32)
    total = mixed[:QUERIES]
    for h in range(1, QUAD):
        total = total + mixed[h * QUERIES : (h + 1) * QUERIES]
    dq[own, :] = (total * HEAD**-0.5).astype(jnp.bfloat16)


def feature_order(block):
    row = lax.broadcasted_iota(jnp.int32, (256, D), 0) + block * 256
    col = lax.broadcasted_iota(jnp.int32, (256, D), 1)
    r = row & 7
    xlo = (row >> 3) & 1
    xhi = (row >> 4) & 1
    y = (row >> 5) & 3
    z = (row >> 7) & 3
    core = row >> 9
    source = (((((xlo * 4 + y) * 2 + xhi) * 4 + z) * 2 + core) << 3) + r
    return jnp.where(col == source, 1.0, 0.0).astype(jnp.bfloat16)


def attention_kernel(
    scale, unroll, x, go, wq, wk, wv, gw, gi, q, k, v, dq, dk, dv, bias, same, xt, total
):
    g = pl.program_id(0)
    band_start = lax.axis_index("lat") * LAT_DEV
    total_rows = LAT_DEV * lax.axis_size("lat")
    first_band = lax.axis_index("lat") == 0
    last_band = lax.axis_index("lat") == lax.axis_size("lat") - 1

    @pl.when(g == 0)
    def _():
        @pl.loop(0, TILES)
        def _(t):
            top = key_tile(t, first_band, last_band)
            bias[t, :KEYS_A, :] = window_bias(t, top, KEYS_A, False, band_start, total_rows)
            bias[t, KEYS_A:, :] = window_bias(t, top, KEYS_B, True, band_start, total_rows)

        row = lax.broadcasted_iota(jnp.int32, (WIDTH, WIDTH), 0)
        col = lax.broadcasted_iota(jnp.int32, (WIDTH, WIDTH), 1)
        same[...] = jnp.where((row >> 6) == (col >> 6), 1.0, 0.0).astype(jnp.bfloat16)

        @pl.loop(0, 4)
        def _(b):
            rows = pl.ds(b * 256, 256)
            xt[rows, :] = mm(feature_order(b), x[...], NT).astype(jnp.bfloat16)

    q[...] = (mm(x[OWN : OWN + OWN_N, :], wq[...]).astype(jnp.bfloat16)) * jnp.bfloat16(0.125)
    k[...] = mm(x[...], wk[...]).astype(jnp.bfloat16)
    v[...] = mm(x[...], wv[...]).astype(jnp.bfloat16)
    dk[...] = jnp.zeros_like(dk)
    dv[...] = jnp.zeros_like(dv)
    if unroll == TILES:
        for t in range(TILES):
            attend(t, key_tile(t, first_band, last_band), q, k, v, go, bias, same, dk, dv, dq)
    else:
        @pl.loop(0, TILES, unroll=unroll)
        def _(t):
            attend(t, key_tile(t, first_band, last_band), q, k, v, go, bias, same, dk, dv, dq)
    dkb = dk[...].astype(jnp.bfloat16)
    dvb = dv[...].astype(jnp.bfloat16)
    gw[0, 0] = (mm(xt[:, OWN : OWN + OWN_N], dq[...]) * scale).astype(jnp.bfloat16)
    gw[0, 1] = (mm(xt[...], dkb) * scale).astype(jnp.bfloat16)
    gw[0, 2] = (mm(xt[...], dvb) * scale).astype(jnp.bfloat16)
    part = mm(
        jnp.concatenate([dkb, dvb], axis=1), jnp.concatenate([wk[...], wv[...]], axis=1), NT
    )

    @pl.when(g == 0)
    def _():
        total[...] = part

    @pl.when(g > 0)
    def _():
        total[...] += part

    total[OWN : OWN + OWN_N, :] += mm(dq[...], wq[...], NT)

    @pl.when(g == pl.num_programs(0) - 1)
    def _():
        gi[...] = total[...]


def attention(x, go, w, scale, unroll=2):
    quads = D // WIDTH
    scratch = [
        pltpu.VMEM((OWN_N, WIDTH), jnp.bfloat16),
        pltpu.VMEM((TOKENS, WIDTH), jnp.bfloat16),
        pltpu.VMEM((TOKENS, WIDTH), jnp.bfloat16),
        pltpu.VMEM((OWN_N, WIDTH), jnp.bfloat16),
        pltpu.VMEM((TOKENS, WIDTH), jnp.float32),
        pltpu.VMEM((TOKENS, WIDTH), jnp.float32),
        pltpu.VMEM((TILES, KEYS, WIDTH), jnp.float32),
        pltpu.VMEM((WIDTH, WIDTH), jnp.bfloat16),
        pltpu.VMEM((D, TOKENS), jnp.bfloat16),
        pltpu.VMEM((TOKENS, D), jnp.float32),
    ]
    return pl.pallas_call(
        functools.partial(attention_kernel, scale, unroll),
        grid=(quads,),
        in_specs=[
            pl.BlockSpec((TOKENS, D), lambda g: (0, 0)),
            pl.BlockSpec((OWN_N, WIDTH), lambda g: (0, g)),
            pl.BlockSpec((D, WIDTH), lambda g: (0, g)),
            pl.BlockSpec((D, WIDTH), lambda g: (0, quads + g)),
            pl.BlockSpec((D, WIDTH), lambda g: (0, 2 * quads + g)),
        ],
        out_specs=[
            pl.BlockSpec((1, 3, D, WIDTH), lambda g: (g, 0, 0, 0)),
            pl.BlockSpec((TOKENS, D), lambda g: (0, 0)),
        ],
        out_shape=[
            jax.ShapeDtypeStruct((quads, 3, D, WIDTH), jnp.bfloat16),
            jax.ShapeDtypeStruct((TOKENS, D), jnp.float32),
        ],
        scratch_shapes=scratch,
        compiler_params=pltpu.CompilerParams(vmem_limit_bytes=60 * 2**20),
        name="attention",
    )(x, go, w, w, w)


def shifted(block, axis, by, wrap):
    size = lax.axis_size(axis)
    route = [(i, (i + by) % size) for i in range(size) if wrap or 0 <= i + by < size]
    return lax.ppermute(block, axis, route)


def extended(inputs):
    x = inputs[0]
    above = shifted(x[-MARGIN:], "lat", 1, False)
    below = shifted(x[:MARGIN], "lat", -1, False)
    tall = jnp.concatenate([above, x, below], axis=0)
    left = shifted(tall[:, -MARGIN:], "lon", 1, True)
    right = shifted(tall[:, :MARGIN], "lon", -1, True)
    sides = jnp.concatenate([left, right], axis=1).reshape(-1, D)
    lead = jnp.zeros((PAD_ROWS * LON_DEV, D), x.dtype)
    end = jnp.zeros((TOKENS - SPLIT - sides.shape[0], D), x.dtype)
    return jnp.concatenate([lead, tall.reshape(-1, D), sides, end], axis=0)


def given_back(gi):
    main = gi[PAD_ROWS * LON_DEV : SPLIT].reshape(LAT_DEV + SIDE, LON_DEV, D)
    sides = gi[SPLIT : SPLIT + (LAT_DEV + SIDE) * SIDE].reshape(LAT_DEV + SIDE, SIDE, D)
    sides = sides.astype(jnp.bfloat16)
    from_right = shifted(sides[:, :MARGIN], "lon", -1, True)
    from_left = shifted(sides[:, MARGIN:], "lon", 1, True)
    extra = jnp.concatenate(
        [from_left, jnp.zeros((LAT_DEV + SIDE, LON_DEV - SIDE, D), jnp.bfloat16), from_right], axis=1
    )
    main = main + extra.astype(jnp.float32)
    from_below = shifted(main[:MARGIN].astype(jnp.bfloat16), "lat", -1, False)
    from_above = shifted(main[-MARGIN:].astype(jnp.bfloat16), "lat", 1, False)
    extra = jnp.concatenate(
        [from_above, jnp.zeros((LAT_DEV - SIDE, LON_DEV, D), jnp.bfloat16), from_below], axis=0
    )
    return main[MARGIN:-MARGIN] + extra.astype(jnp.float32)


STAGES = (2, 4, 4, 4)
LEFT = (512, 128, 32, 8)


def place():
    lon = lax.axis_index("lon")
    return lax.axis_index("dp"), lax.axis_index("lat"), lon >> 3, (lon >> 1) & 3, lon & 1


def device(xlo, y, xhi, z, core):
    return (xlo, y, xhi * 8 + z * 2 + core)


def peers(stage):
    xlo, y, xhi, z, core = place()
    if stage == 0:
        return core, [(1 - core, device(xlo, y, xhi, z, 1 - core))]
    me = (None, z, y, xhi * 2 + xlo)[stage]
    others = []
    for step in (1, 3, 2):
        to = (me + step) & 3
        if stage == 1:
            others.append((to, device(xlo, y, xhi, to, core)))
        elif stage == 2:
            others.append((to, device(xlo, to, xhi, z, core)))
        else:
            others.append((to, device(to & 1, y, to >> 1, z, core)))
    return me, others


def reduce_kernel(quads, part, out, held1, held2, held3, got0, got1, got2, got3, send, recv):
    held = (part, held1, held2, held3)
    got = (got0, got1, got2, got3)
    barrier = pltpu.get_barrier_semaphore()
    count = 0
    for stage in range(4):
        for _, dev in peers(stage)[1]:
            pl.semaphore_signal(barrier, inc=1, device_id=dev, device_id_type=MESH)
            count += 1
    pl.semaphore_wait(barrier, count)

    def copies(c, stage):
        _, others = peers(stage)
        return [
            pltpu.make_async_remote_copy(
                src_ref=held[stage].at[c, :, pl.ds(to * LEFT[stage], LEFT[stage]), :],
                dst_ref=got[stage].at[c, n],
                send_sem=send.at[c, stage, n],
                recv_sem=recv.at[c, stage, n],
                device_id=dev,
                device_id_type=MESH,
            )
            for n, (to, dev) in enumerate(others)
        ]

    def finish(c, stage):
        for copy in copies(c, stage):
            copy.wait()
        me, others = peers(stage)
        rows = pl.ds(pl.multiple_of(me * LEFT[stage], LEFT[stage]), LEFT[stage])
        value = held[stage][c, :, rows, :].astype(jnp.float32)
        for n in range(len(others)):
            value = value + got[stage][c, n].astype(jnp.float32)
        if stage == 3:
            out[c] = value
        else:
            held[stage + 1][c] = value.astype(held[stage + 1].dtype)

    for tick in range(quads + 4):
        for stage in range(4, -1, -1):
            c = tick - stage
            if 0 <= c < quads:
                if stage > 0:
                    finish(c, stage - 1)
                if stage < 4:
                    for copy in copies(c, stage):
                        copy.start()


def reduced(part):
    quads = part.shape[0]
    kinds = (jnp.bfloat16, jnp.bfloat16, jnp.bfloat16, jnp.float32)
    held = [pltpu.VMEM((quads, 3, LEFT[s - 1], WIDTH), kinds[s]) for s in range(1, 4)]
    got = [pltpu.VMEM((quads, STAGES[s] - 1, 3, LEFT[s], WIDTH), kinds[s]) for s in range(4)]
    sems = [pltpu.SemaphoreType.DMA((quads, 4, 3)), pltpu.SemaphoreType.DMA((quads, 4, 3))]
    return pl.pallas_call(
        functools.partial(reduce_kernel, quads),
        out_shape=jax.ShapeDtypeStruct((quads, 3, 8, WIDTH), jnp.float32),
        in_specs=[pl.BlockSpec(memory_space=pltpu.VMEM)],
        out_specs=pl.BlockSpec(memory_space=pltpu.VMEM),
        scratch_shapes=held + got + sems,
        compiler_params=pltpu.CompilerParams(
            collective_id=0, has_side_effects=True, vmem_limit_bytes=40 * 2**20
        ),
        name="reduce_weights",
    )(part)


def body(inputs, grad_out, w_qkv):
    scale = float(2 * 128 * 256) ** -0.5
    x = extended(inputs)
    gw, gi = attention(x, grad_out.reshape(OWN_N, D), w_qkv, scale)
    grad_inputs = given_back(gi).astype(jnp.bfloat16)[None]
    out = reduced(gw)
    grad_w = out.transpose(2, 1, 0, 3).reshape(8, 3 * D)
    return grad_inputs, grad_w


def solution(mesh):
    in_specs = (P("dp", "lat", "lon", None), P("dp", "lat", "lon", None), P())
    out_specs = (P("dp", "lat", "lon", None), P(("dp", "lat", "lon"), None))
    return jax.shard_map(body, mesh=mesh, in_specs=in_specs, out_specs=out_specs, check_vma=False)
```

```python
import functools

import jax
import jax.numpy as jnp
import numpy as np
from jax import lax
from jax.experimental import pallas as pl
from jax.experimental.pallas import tpu as pltpu
from jax.sharding import PartitionSpec as P

WIN = 13
MARGIN = WIN // 2
HEAD = 64
QUAD = 4
WIDTH = QUAD * HEAD
LAT_DEV = 32
LON_DEV = 16
ROW_T = 4
TILES = LAT_DEV // ROW_T
QUERIES = ROW_T * LON_DEV
KEY_ROWS = ROW_T + WIN - 1
SIDE = 2 * MARGIN
KEYS_A = KEY_ROWS * LON_DEV
KEYS_B = KEY_ROWS * SIDE
KEYS = KEYS_A + KEYS_B
PAD_ROWS = 2
OWN = (PAD_ROWS + MARGIN) * LON_DEV
OWN_N = LAT_DEV * LON_DEV
SPLIT = (PAD_ROWS + LAT_DEV + SIDE) * LON_DEV
TOKENS = 1280
D = 1024
NT = (((1,), (1,)), ((), ()))
TN = (((0,), (0,)), ((), ()))
NN = (((1,), (0,)), ((), ()))
MESH = pl.DeviceIdType.MESH


def mm(a, b, dims=NN):
    return lax.dot_general(a, b, dims, preferred_element_type=jnp.float32)


def key_tile(t, first_band, last_band):
    lead = jnp.logical_and(first_band, t == 0).astype(jnp.int32)
    tail = jnp.logical_and(last_band, t == TILES - 1).astype(jnp.int32)
    return t + lead - tail


def window_bias(t, top, keys, side, band_start, total_rows):
    kk = lax.broadcasted_iota(jnp.int32, (keys, WIDTH), 0)
    qq = lax.broadcasted_iota(jnp.int32, (keys, WIDTH), 1) & (QUERIES - 1)
    i, j = qq >> 4, qq & 15
    if side:
        r = (kk * 171) >> 11
        c = kk - r * SIDE
        col = jnp.where(c < MARGIN, c - MARGIN, c + (LON_DEV - MARGIN))
    else:
        r, col = kk >> 4, kk & 15
    first = band_start + ROW_T * t
    key_row = band_start + ROW_T * top - MARGIN + r
    start = jnp.clip(first + i - MARGIN, 0, total_rows - WIN)
    off = key_row - start
    away = col - j
    inside = (off >= 0) & (off < WIN) & (away >= -MARGIN) & (away <= MARGIN)
    return jnp.where(inside, 0.0, -1e30).astype(jnp.float32)


def spread(tile, same_head):
    return jnp.concatenate([tile] * QUAD, axis=0) * same_head


def attend(t, top, cols, q, kv, vv, go, bias, same, dk, dv, dq):
    own = pl.ds(t * QUERIES, QUERIES)
    ka = pl.ds(pl.multiple_of(PAD_ROWS * LON_DEV + top * QUERIES, 32), KEYS_A)
    kb = pl.ds(pl.multiple_of(SPLIT + top * ROW_T * SIDE, 16), KEYS_B)
    same_head = same[...]
    bq = spread(q[own, cols], same_head)
    bg = spread(go[own, cols], same_head)
    keys_a, keys_b = kv[ka, cols], kv[kb, cols]
    sa = mm(keys_a, bq, NT) + bias[t, :KEYS_A, :]
    sb = mm(keys_b, bq, NT) + bias[t, KEYS_A:, :]
    peak = jnp.maximum(jnp.max(sa, axis=0, keepdims=True), jnp.max(sb, axis=0, keepdims=True))
    pa = jnp.exp(sa - peak)
    pb = jnp.exp(sb - peak)
    da = mm(vv[ka, cols], bg, NT)
    db = mm(vv[kb, cols], bg, NT)
    inv = 1.0 / (jnp.sum(pa, axis=0, keepdims=True) + jnp.sum(pb, axis=0, keepdims=True))
    delta = (
        jnp.sum(pa * da, axis=0, keepdims=True) + jnp.sum(pb * db, axis=0, keepdims=True)
    ) * inv
    pa = pa * inv
    pb = pb * inv
    aa = pa.astype(jnp.bfloat16)
    ab = pb.astype(jnp.bfloat16)
    ea = (pa * (da - delta)).astype(jnp.bfloat16)
    eb = (pb * (db - delta)).astype(jnp.bfloat16)
    dk[ka, :] += mm(ea, bq)
    dk[kb, :] += mm(eb, bq)
    dv[ka, :] += mm(aa, bg)
    dv[kb, :] += mm(ab, bg)
    mixed = (mm(ea, keys_a, TN) + mm(eb, keys_b, TN)) * same_head.astype(jnp.float32)
    total = mixed[:QUERIES]
    for h in range(1, QUAD):
        total = total + mixed[h * QUERIES : (h + 1) * QUERIES]
    rows = pl.ds(OWN + t * QUERIES, QUERIES)
    dq[rows, cols] = (total * HEAD**-0.5).astype(jnp.bfloat16)


def feature_order(block):
    row = lax.broadcasted_iota(jnp.int32, (256, D), 0) + block * 256
    col = lax.broadcasted_iota(jnp.int32, (256, D), 1)
    r = row & 7
    xlo = (row >> 3) & 1
    xhi = (row >> 4) & 1
    y = (row >> 5) & 3
    z = (row >> 7) & 3
    core = row >> 9
    source = (((((xlo * 4 + y) * 2 + xhi) * 4 + z) * 2 + core) << 3) + r
    return jnp.where(col == source, 1.0, 0.0).astype(jnp.bfloat16)


STAGES = (2, 4, 4, 4)
LEFT = (512, 128, 32, 8)


def place():
    lon = lax.axis_index("lon")
    return lax.axis_index("dp"), lax.axis_index("lat"), lon >> 3, (lon >> 1) & 3, lon & 1


def device(xlo, y, xhi, z, core):
    return (xlo, y, xhi * 8 + z * 2 + core)


def peers(stage):
    xlo, y, xhi, z, core = place()
    if stage == 0:
        return core, [(1 - core, device(xlo, y, xhi, z, 1 - core))]
    me = (None, z, y, xhi * 2 + xlo)[stage]
    others = []
    for step in (1, 3, 2):
        to = (me + step) & 3
        if stage == 1:
            others.append((to, device(xlo, y, xhi, to, core)))
        elif stage == 2:
            others.append((to, device(xlo, to, xhi, z, core)))
        else:
            others.append((to, device(to & 1, y, to >> 1, z, core)))
    return me, others


SLOTS = ((0, 192, 0, -1), (192, 192, 0, 1), (384, 48, -1, -1), (432, 48, -1, 1), (480, 48, 1, -1), (528, 48, 1, 1))
OPPOSITE = (1, 0, 5, 4, 3, 2)
PACKED = 576
SIDES = TOKENS - SPLIT
ABOVE = PAD_ROWS * LON_DEV
BELOW = OWN + OWN_N
BAND = MARGIN * LON_DEV
QUADS = D // WIDTH


def packing():
    pack = np.zeros((PACKED, OWN_N), np.float32)
    side = np.zeros((SIDES, PACKED), np.float32)
    for start, size, dy, dx in SLOTS:
        count = LAT_DEV if dy == 0 else MARGIN
        for r in range(count):
            for c in range(MARGIN):
                row = r + (LAT_DEV - MARGIN if dy > 0 else 0)
                col = c + (LON_DEV - MARGIN if dx > 0 else 0)
                pack[start + r * MARGIN + c, row * LON_DEV + col] = 1
                row = r + (MARGIN if dy == 0 else 0 if dy < 0 else LAT_DEV + MARGIN)
                col = c + (MARGIN if dx > 0 else 0)
                side[row * SIDE + col, start + r * MARGIN + c] = 1
    return jnp.asarray(pack, jnp.bfloat16), jnp.asarray(side, jnp.bfloat16)


def fused_kernel(
    scale, x, pack, go_hbm, w_hbm, side_hbm, gi, gw,
    go, w, side, xe, packed, halo, q, k, v, dall, dk, dv, bias, same, xt,
    part, held1, held2, held3, got0, got1, got2, got3,
    edge, back, lat_out, lat_in, own_grad,
    load, send, recv, halo_send, halo_recv, back_send, back_recv,
):
    dp, lat, lon = lax.axis_index("dp"), lax.axis_index("lat"), lax.axis_index("lon")
    lats, lons = lax.axis_size("lat"), lax.axis_size("lon")
    band_start = lat * LAT_DEV
    total_rows = LAT_DEV * lats
    first_band, last_band = lat == 0, lat == lats - 1
    held = (part, held1, held2, held3)
    got = (got0, got1, got2, got3)

    loads = [
        pltpu.make_async_copy(w_hbm, w, load.at[0]),
        pltpu.make_async_copy(go_hbm, go, load.at[1]),
        pltpu.make_async_copy(side_hbm, side, load.at[2]),
    ]
    for copy in loads:
        copy.start()

    def when_there(dy, act):
        if dy == 0:
            act()
        else:
            pl.when(lat > 0 if dy < 0 else lat < lats - 1)(act)

    def neighbour(dy, dx):
        return (dp, lat + dy, lax.rem(lon + dx + lons, lons))

    moves = [(dy, dx) for _, _, dy, dx in SLOTS] + [(-1, 0), (1, 0)]

    packed[...] = mm(pack[...], x[...]).astype(jnp.bfloat16)

    barrier = pltpu.get_barrier_semaphore()
    count = 0
    for stage in range(4):
        for _, dev in peers(stage)[1]:
            pl.semaphore_signal(barrier, inc=1, device_id=dev, device_id_type=MESH)
            count += 1
    for dy, dx in moves:
        @functools.partial(when_there, dy)
        def _():
            pl.semaphore_signal(barrier, inc=1, device_id=neighbour(dy, dx), device_id_type=MESH)
    count = count + 2 + 3 * (lat > 0).astype(jnp.int32) + 3 * (lat < lats - 1).astype(jnp.int32)
    pl.semaphore_wait(barrier, count)

    def exchange(source, target, up, down, into_up, into_down, sends, recvs, sending):
        for n, (dy, dx) in enumerate(moves):
            @functools.partial(when_there, dy)
            def _():
                if n < 6:
                    other = OPPOSITE[n]
                    start, size = SLOTS[n][:2]
                    there = SLOTS[other][0]
                    src = source.at[pl.ds(start, size), :]
                    far, near = target.at[pl.ds(there, size), :], target.at[pl.ds(start, size), :]
                else:
                    other = 13 - n
                    src = (up, down)[n - 6]
                    far, near = (into_down, into_up) if n == 6 else (into_up, into_down)
                copy = pltpu.make_async_remote_copy(
                    src_ref=src,
                    dst_ref=far if sending else near,
                    send_sem=sends.at[n],
                    recv_sem=recvs.at[other if sending else n],
                    device_id=neighbour(dy, dx),
                    device_id_type=MESH,
                )
                if sending:
                    copy.start()
                else:
                    copy.wait()

    def halo_exchange(sending):
        exchange(
            packed, halo, x.at[pl.ds(0, BAND), :], x.at[pl.ds(OWN_N - BAND, BAND), :],
            xe.at[pl.ds(ABOVE, BAND), :], xe.at[pl.ds(BELOW, BAND), :],
            halo_send, halo_recv, sending,
        )

    def give_back(sending):
        exchange(
            edge, back, lat_out.at[pl.ds(0, BAND), :], lat_out.at[pl.ds(BAND, BAND), :],
            lat_in.at[pl.ds(0, BAND), :], lat_in.at[pl.ds(BAND, BAND), :],
            back_send, back_recv, sending,
        )

    halo_exchange(True)

    for there, slot in ((lat > 0, 384), (lat < lats - 1, 480)):
        @pl.when(jnp.logical_not(there))
        def _():
            zero = jnp.zeros((96, D), jnp.bfloat16)
            halo[slot : slot + 96, :] = zero
            back[slot : slot + 96, :] = zero
            at = ABOVE if slot == 384 else BELOW
            xe[at : at + BAND, :] = zero
            at = 0 if slot == 384 else BAND
            lat_in[at : at + BAND, :] = zero

    xe[:ABOVE, :] = jnp.zeros((ABOVE, D), jnp.bfloat16)
    xe[OWN : OWN + OWN_N, :] = x[...]
    row = lax.broadcasted_iota(jnp.int32, (WIDTH, WIDTH), 0)
    col = lax.broadcasted_iota(jnp.int32, (WIDTH, WIDTH), 1)
    same[...] = jnp.where((row >> 6) == (col >> 6), 1.0, 0.0).astype(jnp.bfloat16)

    loads[0].wait()

    @pl.loop(0, QUADS)
    def _(b):
        cols = pl.ds(pl.multiple_of(b * WIDTH, WIDTH), WIDTH)
        kcols = pl.ds(pl.multiple_of(D + b * WIDTH, WIDTH), WIDTH)
        vcols = pl.ds(pl.multiple_of(2 * D + b * WIDTH, WIDTH), WIDTH)
        q[:, cols] = mm(x[...], w[:, cols]).astype(jnp.bfloat16) * jnp.bfloat16(0.125)
        k[OWN : OWN + OWN_N, cols] = mm(x[...], w[:, kcols]).astype(jnp.bfloat16)
        v[OWN : OWN + OWN_N, cols] = mm(x[...], w[:, vcols]).astype(jnp.bfloat16)

    @pl.loop(0, TILES)
    def _(t):
        top = key_tile(t, first_band, last_band)
        bias[t, :KEYS_A, :] = window_bias(t, top, KEYS_A, False, band_start, total_rows)
        bias[t, KEYS_A:, :] = window_bias(t, top, KEYS_B, True, band_start, total_rows)

    loads[1].wait()
    loads[2].wait()
    halo_exchange(False)
    xe[SPLIT:, :] = mm(side[...], halo[...]).astype(jnp.bfloat16)

    @pl.loop(0, QUADS)
    def _(b):
        cols = pl.ds(pl.multiple_of(b * WIDTH, WIDTH), WIDTH)
        kcols = pl.ds(pl.multiple_of(D + b * WIDTH, WIDTH), WIDTH)
        vcols = pl.ds(pl.multiple_of(2 * D + b * WIDTH, WIDTH), WIDTH)
        outer = jnp.concatenate([xe[:OWN, :], xe[BELOW:, :]], axis=0)
        for into, wcols in ((k, kcols), (v, vcols)):
            value = mm(outer, w[:, wcols]).astype(jnp.bfloat16)
            into[:OWN, cols] = value[:OWN]
            into[BELOW:, cols] = value[OWN:]
        rows = pl.ds(pl.multiple_of(b * 256, 256), 256)
        xt[rows, :] = mm(feature_order(b), xe[...], NT).astype(jnp.bfloat16)

    def copies(c, stage):
        return [
            pltpu.make_async_remote_copy(
                src_ref=held[stage].at[c, :, pl.ds(to * LEFT[stage], LEFT[stage]), :],
                dst_ref=got[stage].at[c, n],
                send_sem=send.at[c, stage, n],
                recv_sem=recv.at[c, stage, n],
                device_id=dev,
                device_id_type=MESH,
            )
            for n, (to, dev) in enumerate(peers(stage)[1])
        ]

    def begin(c, stage):
        for copy in copies(c, stage):
            copy.start()

    def finish(c, stage):
        for copy in copies(c, stage):
            copy.wait()
        me, others = peers(stage)
        rows = pl.ds(pl.multiple_of(me * LEFT[stage], LEFT[stage]), LEFT[stage])
        for i in range(3):
            value = held[stage][c, i, rows, :].astype(jnp.float32)
            for n in range(len(others)):
                value = value + got[stage][c, n, i].astype(jnp.float32)
            if stage == 3:
                at = i * D + c * WIDTH
                gw[:, pl.ds(at if isinstance(at, int) else pl.multiple_of(at, WIDTH), WIDTH)] = value
            else:
                held[stage + 1][c, i] = value.astype(held[stage + 1].dtype)
        if stage < 3:
            begin(c, stage + 1)

    @pl.loop(0, QUADS)
    def _(g):
        cols = pl.ds(pl.multiple_of(g * WIDTH, WIDTH), WIDTH)
        kcols = pl.ds(pl.multiple_of(D + g * WIDTH, WIDTH), WIDTH)
        vcols = pl.ds(pl.multiple_of(2 * D + g * WIDTH, WIDTH), WIDTH)
        dk[...] = jnp.zeros_like(dk)
        dv[...] = jnp.zeros_like(dv)

        def tiles(a, b):
            for t in range(a, b):
                top = key_tile(t, first_band, last_band)
                attend(t, top, cols, q, k, v, go, bias, same, dk, dv, dall)

        tiles(0, 4)

        @pl.when(g >= 1)
        def _():
            finish(g - 1, 0)

        tiles(4, TILES)

        @pl.when(g >= 2)
        def _():
            finish(g - 2, 2)

        dall[:, kcols] = dk[...].astype(jnp.bfloat16)
        dall[:, vcols] = dv[...].astype(jnp.bfloat16)
        mine = pl.ds(OWN, OWN_N)
        part[g, 0] = (mm(xt[:, mine], dall[mine, cols]) * scale).astype(jnp.bfloat16)
        part[g, 1] = (mm(xt[...], dall[:, kcols]) * scale).astype(jnp.bfloat16)
        part[g, 2] = (mm(xt[...], dall[:, vcols]) * scale).astype(jnp.bfloat16)
        begin(g, 0)

        @pl.when(g >= 1)
        def _():
            finish(g - 1, 1)

        @pl.when(g >= 2)
        def _():
            finish(g - 2, 3)

    @pl.loop(0, QUADS)
    def _(b):
        cols = pl.ds(pl.multiple_of(b * WIDTH, WIDTH), WIDTH)
        rows = jnp.concatenate([dall[ABOVE:OWN, D:], dall[BELOW:, D:]], axis=0)
        value = mm(rows, w[cols, D:], NT).astype(jnp.bfloat16)
        lat_out[:, cols] = value[: 2 * BAND]
        edge[:, cols] = mm(side[...], value[2 * BAND :], TN).astype(jnp.bfloat16)

    give_back(True)
    finish(3, 0)
    finish(2, 2)

    @pl.loop(0, QUADS)
    def _(b):
        cols = pl.ds(pl.multiple_of(b * WIDTH, WIDTH), WIDTH)
        own_grad[:, cols] = mm(dall[OWN:BELOW, :], w[cols, :], NT)

    finish(2, 3)
    finish(3, 1)
    give_back(False)

    @pl.loop(0, QUADS)
    def _(b):
        cols = pl.ds(pl.multiple_of(b * WIDTH, WIDTH), WIDTH)
        value = own_grad[:, cols] + mm(pack[...], back[:, cols], TN)
        gi[:, cols] = value.astype(jnp.bfloat16)
        gi[:BAND, cols] = (value[:BAND] + lat_in[:BAND, cols].astype(jnp.float32)).astype(jnp.bfloat16)
        gi[OWN_N - BAND :, cols] = (
            value[OWN_N - BAND :] + lat_in[BAND:, cols].astype(jnp.float32)
        ).astype(jnp.bfloat16)

    finish(3, 2)
    finish(3, 3)


def fused(x, go, w, scale):
    bf, f32 = jnp.bfloat16, jnp.float32
    kinds = (bf, bf, bf, f32)
    pack, side = packing()
    scratch = [
        pltpu.VMEM((OWN_N, D), bf),
        pltpu.VMEM((D, 3 * D), bf),
        pltpu.VMEM((SIDES, PACKED), bf),
        pltpu.VMEM((TOKENS, D), bf),
        pltpu.VMEM((PACKED, D), bf),
        pltpu.VMEM((PACKED, D), bf),
        pltpu.VMEM((OWN_N, D), bf),
        pltpu.VMEM((TOKENS, D), bf),
        pltpu.VMEM((TOKENS, D), bf),
        pltpu.VMEM((TOKENS, 3 * D), bf),
        pltpu.VMEM((TOKENS, WIDTH), f32),
        pltpu.VMEM((TOKENS, WIDTH), f32),
        pltpu.VMEM((TILES, KEYS, WIDTH), f32),
        pltpu.VMEM((WIDTH, WIDTH), bf),
        pltpu.VMEM((D, TOKENS), bf),
        pltpu.VMEM((QUADS, 3, D, WIDTH), bf),
    ]
    scratch += [pltpu.VMEM((QUADS, 3, LEFT[s - 1], WIDTH), kinds[s]) for s in range(1, 4)]
    scratch += [pltpu.VMEM((QUADS, STAGES[s] - 1, 3, LEFT[s], WIDTH), kinds[s]) for s in range(4)]
    scratch += [
        pltpu.VMEM((PACKED, D), bf),
        pltpu.VMEM((PACKED, D), bf),
        pltpu.VMEM((2 * BAND, D), bf),
        pltpu.VMEM((2 * BAND, D), bf),
        pltpu.VMEM((OWN_N, D), f32),
        pltpu.SemaphoreType.DMA((3,)),
        pltpu.SemaphoreType.DMA((QUADS, 4, 3)),
        pltpu.SemaphoreType.DMA((QUADS, 4, 3)),
        pltpu.SemaphoreType.DMA((8,)),
        pltpu.SemaphoreType.DMA((8,)),
        pltpu.SemaphoreType.DMA((8,)),
        pltpu.SemaphoreType.DMA((8,)),
    ]
    vmem = pl.BlockSpec(memory_space=pltpu.VMEM)
    anywhere = pl.BlockSpec(memory_space=pl.ANY)
    return pl.pallas_call(
        functools.partial(fused_kernel, scale),
        out_shape=[
            jax.ShapeDtypeStruct((OWN_N, D), bf),
            jax.ShapeDtypeStruct((8, 3 * D), f32),
        ],
        in_specs=[vmem, vmem, anywhere, anywhere, anywhere],
        out_specs=[vmem, vmem],
        scratch_shapes=scratch,
        compiler_params=pltpu.CompilerParams(
            collective_id=0, has_side_effects=True, vmem_limit_bytes=61 * 2**20
        ),
        name="attention_backward",
    )(x, pack, go, w, side)


def body(inputs, grad_out, w_qkv):
    scale = float(2 * 128 * 256) ** -0.5
    gi, gw = fused(inputs.reshape(OWN_N, D), grad_out.reshape(OWN_N, D), w_qkv, scale)
    return gi.reshape(inputs.shape), gw


def solution(mesh):
    in_specs = (P("dp", "lat", "lon", None), P("dp", "lat", "lon", None), P())
    out_specs = (P("dp", "lat", "lon", None), P(("dp", "lat", "lon"), None))
    return jax.shard_map(body, mesh=mesh, in_specs=in_specs, out_specs=out_specs, check_vma=False)
```

```python
import functools

import jax
import jax.numpy as jnp
import numpy as np
from jax import lax
from jax.experimental import pallas as pl
from jax.experimental.pallas import tpu as pltpu
from jax.sharding import PartitionSpec as P

WIN = 13
MARGIN = WIN // 2
HEAD = 64
QUAD = 4
WIDTH = QUAD * HEAD
LAT_DEV = 32
LON_DEV = 16
ROW_T = 4
TILES = LAT_DEV // ROW_T
QUERIES = ROW_T * LON_DEV
KEY_ROWS = ROW_T + WIN - 1
SIDE = 2 * MARGIN
KEYS_A = KEY_ROWS * LON_DEV
KEYS_B = KEY_ROWS * SIDE
KEYS = KEYS_A + KEYS_B
PAD_ROWS = 2
OWN = (PAD_ROWS + MARGIN) * LON_DEV
OWN_N = LAT_DEV * LON_DEV
SPLIT = (PAD_ROWS + LAT_DEV + SIDE) * LON_DEV
TOKENS = 1280
D = 1024
NT = (((1,), (1,)), ((), ()))
TN = (((0,), (0,)), ((), ()))
NN = (((1,), (0,)), ((), ()))
MESH = pl.DeviceIdType.MESH


def mm(a, b, dims=NN):
    return lax.dot_general(a, b, dims, preferred_element_type=jnp.float32)


def key_tile(t, first_band, last_band):
    lead = jnp.logical_and(first_band, t == 0).astype(jnp.int32)
    tail = jnp.logical_and(last_band, t == TILES - 1).astype(jnp.int32)
    return t + lead - tail


def window_bias(t, top, keys, side, band_start, total_rows):
    kk = lax.broadcasted_iota(jnp.int32, (keys, WIDTH), 0)
    qq = lax.broadcasted_iota(jnp.int32, (keys, WIDTH), 1) & (QUERIES - 1)
    i, j = qq >> 4, qq & 15
    if side:
        r = (kk * 171) >> 11
        c = kk - r * SIDE
        col = jnp.where(c < MARGIN, c - MARGIN, c + (LON_DEV - MARGIN))
    else:
        r, col = kk >> 4, kk & 15
    first = band_start + ROW_T * t
    key_row = band_start + ROW_T * top - MARGIN + r
    start = jnp.clip(first + i - MARGIN, 0, total_rows - WIN)
    off = key_row - start
    away = col - j
    inside = (off >= 0) & (off < WIN) & (away >= -MARGIN) & (away <= MARGIN)
    return jnp.where(inside, 0.0, -1e30).astype(jnp.float32)


def spread(tile, same_head):
    return jnp.concatenate([tile] * QUAD, axis=0) * same_head


def attend(t, top, cols, q, kv, vv, go, bias, same, dk, dv, dq):
    own = pl.ds(t * QUERIES, QUERIES)
    ka = pl.ds(pl.multiple_of(PAD_ROWS * LON_DEV + top * QUERIES, 32), KEYS_A)
    kb = pl.ds(pl.multiple_of(SPLIT + top * ROW_T * SIDE, 16), KEYS_B)
    kind = min(t, 2) if t < TILES - 2 else t - TILES + 5
    same_head = same[...]
    bq = spread(q[own, cols], same_head)
    bg = spread(go[own, cols], same_head)
    keys_a, keys_b = kv[ka, cols], kv[kb, cols]
    sa = mm(keys_a, bq, NT) + bias[kind, :KEYS_A, :]
    sb = mm(keys_b, bq, NT) + bias[kind, KEYS_A:, :]
    peak = jnp.maximum(jnp.max(sa, axis=0, keepdims=True), jnp.max(sb, axis=0, keepdims=True))
    pa = jnp.exp(sa - peak)
    pb = jnp.exp(sb - peak)
    da = mm(vv[ka, cols], bg, NT)
    db = mm(vv[kb, cols], bg, NT)
    inv = 1.0 / (jnp.sum(pa, axis=0, keepdims=True) + jnp.sum(pb, axis=0, keepdims=True))
    delta = (
        jnp.sum(pa * da, axis=0, keepdims=True) + jnp.sum(pb * db, axis=0, keepdims=True)
    ) * inv
    pa = pa * inv
    pb = pb * inv
    aa = pa.astype(jnp.bfloat16)
    ab = pb.astype(jnp.bfloat16)
    ea = (pa * (da - delta)).astype(jnp.bfloat16)
    eb = (pb * (db - delta)).astype(jnp.bfloat16)
    dk[ka, :] += mm(ea, bq)
    dk[kb, :] += mm(eb, bq)
    dv[ka, :] += mm(aa, bg)
    dv[kb, :] += mm(ab, bg)
    mixed = (mm(ea, keys_a, TN) + mm(eb, keys_b, TN)) * same_head.astype(jnp.float32)
    total = mixed[:QUERIES]
    for h in range(1, QUAD):
        total = total + mixed[h * QUERIES : (h + 1) * QUERIES]
    rows = pl.ds(OWN + t * QUERIES, QUERIES)
    dq[rows, cols] = (total * HEAD**-0.5).astype(jnp.bfloat16)


STAGES = (2, 4, 4, 4)
LEFT = (512, 128, 32, 8)


def place():
    lon = lax.axis_index("lon")
    return lax.axis_index("dp"), lax.axis_index("lat"), lon >> 3, (lon >> 1) & 3, lon & 1


def device(xlo, y, xhi, z, core):
    return (xlo, y, xhi * 8 + z * 2 + core)


ORDERS = ("zyx", "yxz", "xzy")


def along(axis):
    xlo, y, xhi, z, core = place()
    me = {"x": xhi * 2 + xlo, "y": y, "z": z}[axis]
    others = []
    for step in (1, 3, 2):
        to = (me + step) & 3
        if axis == "z":
            others.append((to, device(xlo, y, xhi, to, core)))
        elif axis == "y":
            others.append((to, device(xlo, to, xhi, z, core)))
        else:
            others.append((to, device(to & 1, y, to >> 1, z, core)))
    return me, others


def peers(stage, i):
    if stage == 0:
        xlo, y, xhi, z, core = place()
        return core, [(1 - core, device(xlo, y, xhi, z, 1 - core))]
    return along(ORDERS[i][stage - 1])


def by_owner(value, order):
    blocks = []
    for core in range(2):
        for n in range(64):
            at = dict(zip(order, (n >> 4, (n >> 2) & 3, n & 3)))
            xlo, xhi = at["x"] & 1, at["x"] >> 1
            start = ((((xlo * 4 + at["y"]) * 2 + xhi) * 4 + at["z"]) * 2 + core) * 8
            blocks.append(value[start : start + 8])
    return jnp.concatenate(blocks, axis=0)


SLOTS = ((0, 192, 0, -1), (192, 192, 0, 1), (384, 48, -1, -1), (432, 48, -1, 1), (480, 48, 1, -1), (528, 48, 1, 1))
OPPOSITE = (1, 0, 5, 4, 3, 2)
PACKED = 576
SIDES = TOKENS - SPLIT
ABOVE = PAD_ROWS * LON_DEV
BELOW = OWN + OWN_N
BAND = MARGIN * LON_DEV
QUADS = D // WIDTH


def packing():
    pack = np.zeros((PACKED, OWN_N), np.float32)
    side = np.zeros((SIDES, PACKED), np.float32)
    for start, size, dy, dx in SLOTS:
        count = LAT_DEV if dy == 0 else MARGIN
        for r in range(count):
            for c in range(MARGIN):
                row = r + (LAT_DEV - MARGIN if dy > 0 else 0)
                col = c + (LON_DEV - MARGIN if dx > 0 else 0)
                pack[start + r * MARGIN + c, row * LON_DEV + col] = 1
                row = r + (MARGIN if dy == 0 else 0 if dy < 0 else LAT_DEV + MARGIN)
                col = c + (MARGIN if dx > 0 else 0)
                side[row * SIDE + col, start + r * MARGIN + c] = 1
    return jnp.asarray(pack, jnp.bfloat16), jnp.asarray(side, jnp.bfloat16)


def fused_kernel(
    scale, x, pack, go_hbm, w_hbm, side_hbm, gi, gw,
    go, w, side, xe, packed, halo, q, k, v, dall, dk, dv, bias, same, xt,
    part, held1, held2, held3, got0, got1, got2, got3,
    edge, back, lat_out, lat_in, own_grad,
    load, send, recv, halo_send, halo_recv, back_send, back_recv,
):
    dp, lat, lon = lax.axis_index("dp"), lax.axis_index("lat"), lax.axis_index("lon")
    lats, lons = lax.axis_size("lat"), lax.axis_size("lon")
    band_start = lat * LAT_DEV
    total_rows = LAT_DEV * lats
    first_band, last_band = lat == 0, lat == lats - 1
    held = (part, held1, held2, held3)
    got = (got0, got1, got2, got3)

    loads = [
        pltpu.make_async_copy(w_hbm, w, load.at[0]),
        pltpu.make_async_copy(go_hbm, go, load.at[1]),
        pltpu.make_async_copy(side_hbm, side, load.at[2]),
    ]
    for copy in loads:
        copy.start()

    def when_there(dy, act):
        if dy == 0:
            act()
        else:
            pl.when(lat > 0 if dy < 0 else lat < lats - 1)(act)

    def neighbour(dy, dx):
        return (dp, lat + dy, lax.rem(lon + dx + lons, lons))

    moves = [(dy, dx) for _, _, dy, dx in SLOTS] + [(-1, 0), (1, 0)]

    packed[...] = mm(pack[...], x[...]).astype(jnp.bfloat16)

    barrier = pltpu.get_barrier_semaphore()
    count = 0
    for others in (peers(0, 0)[1], along("x")[1], along("y")[1], along("z")[1]):
        for _, dev in others:
            pl.semaphore_signal(barrier, inc=1, device_id=dev, device_id_type=MESH)
            count += 1
    for dy, dx in moves:
        @functools.partial(when_there, dy)
        def _():
            pl.semaphore_signal(barrier, inc=1, device_id=neighbour(dy, dx), device_id_type=MESH)
    count = count + 2 + 3 * (lat > 0).astype(jnp.int32) + 3 * (lat < lats - 1).astype(jnp.int32)
    pl.semaphore_wait(barrier, count)

    def exchange(source, target, up, down, into_up, into_down, sends, recvs, sending):
        for n, (dy, dx) in enumerate(moves):
            @functools.partial(when_there, dy)
            def _():
                if n < 6:
                    other = OPPOSITE[n]
                    start, size = SLOTS[n][:2]
                    there = SLOTS[other][0]
                    src = source.at[pl.ds(start, size), :]
                    far, near = target.at[pl.ds(there, size), :], target.at[pl.ds(start, size), :]
                else:
                    other = 13 - n
                    src = (up, down)[n - 6]
                    far, near = (into_down, into_up) if n == 6 else (into_up, into_down)
                copy = pltpu.make_async_remote_copy(
                    src_ref=src,
                    dst_ref=far if sending else near,
                    send_sem=sends.at[n],
                    recv_sem=recvs.at[other if sending else n],
                    device_id=neighbour(dy, dx),
                    device_id_type=MESH,
                )
                if sending:
                    copy.start()
                else:
                    copy.wait()

    def halo_exchange(sending):
        exchange(
            packed, halo, x.at[pl.ds(0, BAND), :], x.at[pl.ds(OWN_N - BAND, BAND), :],
            xe.at[pl.ds(ABOVE, BAND), :], xe.at[pl.ds(BELOW, BAND), :],
            halo_send, halo_recv, sending,
        )

    def give_back(sending):
        exchange(
            edge, back, lat_out.at[pl.ds(0, BAND), :], lat_out.at[pl.ds(BAND, BAND), :],
            lat_in.at[pl.ds(0, BAND), :], lat_in.at[pl.ds(BAND, BAND), :],
            back_send, back_recv, sending,
        )

    halo_exchange(True)

    for there, slot in ((lat > 0, 384), (lat < lats - 1, 480)):
        @pl.when(jnp.logical_not(there))
        def _():
            zero = jnp.zeros((96, D), jnp.bfloat16)
            halo[slot : slot + 96, :] = zero
            back[slot : slot + 96, :] = zero
            at = ABOVE if slot == 384 else BELOW
            xe[at : at + BAND, :] = zero
            at = 0 if slot == 384 else BAND
            lat_in[at : at + BAND, :] = zero

    xe[:ABOVE, :] = jnp.zeros((ABOVE, D), jnp.bfloat16)
    xe[OWN : OWN + OWN_N, :] = x[...]
    row = lax.broadcasted_iota(jnp.int32, (WIDTH, WIDTH), 0)
    col = lax.broadcasted_iota(jnp.int32, (WIDTH, WIDTH), 1)
    same[...] = jnp.where((row >> 6) == (col >> 6), 1.0, 0.0).astype(jnp.bfloat16)

    loads[0].wait()

    @pl.loop(0, QUADS)
    def _(b):
        cols = pl.ds(pl.multiple_of(b * WIDTH, WIDTH), WIDTH)
        kcols = pl.ds(pl.multiple_of(D + b * WIDTH, WIDTH), WIDTH)
        vcols = pl.ds(pl.multiple_of(2 * D + b * WIDTH, WIDTH), WIDTH)
        q[:, cols] = mm(x[...], w[:, cols]).astype(jnp.bfloat16) * jnp.bfloat16(0.125)
        k[OWN : OWN + OWN_N, cols] = mm(x[...], w[:, kcols]).astype(jnp.bfloat16)
        v[OWN : OWN + OWN_N, cols] = mm(x[...], w[:, vcols]).astype(jnp.bfloat16)

    @pl.loop(0, 5)
    def _(n):
        t = n + (TILES - 5) * (n >= 3).astype(jnp.int32)
        top = key_tile(t, first_band, last_band)
        bias[n, :KEYS_A, :] = window_bias(t, top, KEYS_A, False, band_start, total_rows)
        bias[n, KEYS_A:, :] = window_bias(t, top, KEYS_B, True, band_start, total_rows)

    loads[1].wait()
    loads[2].wait()
    halo_exchange(False)
    xe[SPLIT:, :] = mm(side[...], halo[...]).astype(jnp.bfloat16)

    @pl.loop(0, QUADS)
    def _(b):
        cols = pl.ds(pl.multiple_of(b * WIDTH, WIDTH), WIDTH)
        kcols = pl.ds(pl.multiple_of(D + b * WIDTH, WIDTH), WIDTH)
        vcols = pl.ds(pl.multiple_of(2 * D + b * WIDTH, WIDTH), WIDTH)
        outer = jnp.concatenate([xe[:OWN, :], xe[BELOW:, :]], axis=0)
        for into, wcols in ((k, kcols), (v, vcols)):
            value = mm(outer, w[:, wcols]).astype(jnp.bfloat16)
            into[:OWN, cols] = value[:OWN]
            into[BELOW:, cols] = value[OWN:]
        rows = pl.ds(pl.multiple_of(b * 256, 256), 256)
        xt[rows, :] = xe[:, rows].T

    def copies(c, stage, i):
        return [
            pltpu.make_async_remote_copy(
                src_ref=held[stage].at[c, i, pl.ds(to * LEFT[stage], LEFT[stage]), :],
                dst_ref=got[stage].at[c, i, n],
                send_sem=send.at[c, stage, i, n],
                recv_sem=recv.at[c, stage, i, n],
                device_id=dev,
                device_id_type=MESH,
            )
            for n, (to, dev) in enumerate(peers(stage, i)[1])
        ]

    def begin(c, stage, i):
        for copy in copies(c, stage, i):
            copy.start()

    def finish(c, stage):
        for i in range(3):
            for copy in copies(c, stage, i):
                copy.wait()
            me, others = peers(stage, i)
            rows = pl.ds(pl.multiple_of(me * LEFT[stage], LEFT[stage]), LEFT[stage])
            value = held[stage][c, i, rows, :].astype(jnp.float32)
            for n in range(len(others)):
                value = value + got[stage][c, i, n].astype(jnp.float32)
            if stage == 3:
                at = i * D + c * WIDTH
                at = at if isinstance(at, int) else pl.multiple_of(at, WIDTH)
                gw[:, pl.ds(at, WIDTH)] = value
            else:
                held[stage + 1][c, i] = value.astype(held[stage + 1].dtype)
                begin(c, stage + 1, i)

    @pl.loop(0, QUADS)
    def _(g):
        cols = pl.ds(pl.multiple_of(g * WIDTH, WIDTH), WIDTH)
        kcols = pl.ds(pl.multiple_of(D + g * WIDTH, WIDTH), WIDTH)
        vcols = pl.ds(pl.multiple_of(2 * D + g * WIDTH, WIDTH), WIDTH)
        dk[...] = jnp.zeros_like(dk)
        dv[...] = jnp.zeros_like(dv)

        def tiles(a, b):
            for t in range(a, b):
                top = key_tile(t, first_band, last_band)
                attend(t, top, cols, q, k, v, go, bias, same, dk, dv, dall)

        tiles(0, 4)

        @pl.when(g >= 1)
        def _():
            finish(g - 1, 0)

        tiles(4, TILES)

        @pl.when(g >= 2)
        def _():
            finish(g - 2, 2)

        dall[:, kcols] = dk[...].astype(jnp.bfloat16)
        dall[:, vcols] = dv[...].astype(jnp.bfloat16)
        mine = pl.ds(OWN, OWN_N)
        for i, tokens, wide in ((0, mine, cols), (1, slice(None), kcols), (2, slice(None), vcols)):
            value = mm(xt[:, tokens], dall[tokens, wide]) * scale
            part[g, i] = by_owner(value, ORDERS[i]).astype(jnp.bfloat16)
            begin(g, 0, i)

        @pl.when(g >= 1)
        def _():
            finish(g - 1, 1)

        @pl.when(g >= 2)
        def _():
            finish(g - 2, 3)

    @pl.loop(0, QUADS)
    def _(b):
        cols = pl.ds(pl.multiple_of(b * WIDTH, WIDTH), WIDTH)
        rows = jnp.concatenate([dall[ABOVE:OWN, D:], dall[BELOW:, D:]], axis=0)
        value = mm(rows, w[cols, D:], NT).astype(jnp.bfloat16)
        lat_out[:, cols] = value[: 2 * BAND]
        edge[:, cols] = mm(side[...], value[2 * BAND :], TN).astype(jnp.bfloat16)

    give_back(True)
    finish(3, 0)
    finish(2, 2)

    @pl.loop(0, QUADS)
    def _(b):
        cols = pl.ds(pl.multiple_of(b * WIDTH, WIDTH), WIDTH)
        own_grad[:, cols] = mm(dall[OWN:BELOW, :], w[cols, :], NT)

    finish(2, 3)
    finish(3, 1)
    give_back(False)

    @pl.loop(0, QUADS)
    def _(b):
        cols = pl.ds(pl.multiple_of(b * WIDTH, WIDTH), WIDTH)
        value = own_grad[:, cols] + mm(pack[...], back[:, cols], TN)
        gi[:, cols] = value.astype(jnp.bfloat16)
        gi[:BAND, cols] = (value[:BAND] + lat_in[:BAND, cols].astype(jnp.float32)).astype(jnp.bfloat16)
        gi[OWN_N - BAND :, cols] = (
            value[OWN_N - BAND :] + lat_in[BAND:, cols].astype(jnp.float32)
        ).astype(jnp.bfloat16)

    finish(3, 2)
    finish(3, 3)


def fused(x, go, w, scale):
    bf, f32 = jnp.bfloat16, jnp.float32
    kinds = (bf, bf, bf, f32)
    pack, side = packing()
    scratch = [
        pltpu.VMEM((OWN_N, D), bf),
        pltpu.VMEM((D, 3 * D), bf),
        pltpu.VMEM((SIDES, PACKED), bf),
        pltpu.VMEM((TOKENS, D), bf),
        pltpu.VMEM((PACKED, D), bf),
        pltpu.VMEM((PACKED, D), bf),
        pltpu.VMEM((OWN_N, D), bf),
        pltpu.VMEM((TOKENS, D), bf),
        pltpu.VMEM((TOKENS, D), bf),
        pltpu.VMEM((TOKENS, 3 * D), bf),
        pltpu.VMEM((TOKENS, WIDTH), f32),
        pltpu.VMEM((TOKENS, WIDTH), f32),
        pltpu.VMEM((5, KEYS, WIDTH), f32),
        pltpu.VMEM((WIDTH, WIDTH), bf),
        pltpu.VMEM((D, TOKENS), bf),
        pltpu.VMEM((QUADS, 3, D, WIDTH), bf),
    ]
    scratch += [pltpu.VMEM((QUADS, 3, LEFT[s - 1], WIDTH), kinds[s]) for s in range(1, 4)]
    scratch += [pltpu.VMEM((QUADS, 3, STAGES[s] - 1, LEFT[s], WIDTH), kinds[s]) for s in range(4)]
    scratch += [
        pltpu.VMEM((PACKED, D), bf),
        pltpu.VMEM((PACKED, D), bf),
        pltpu.VMEM((2 * BAND, D), bf),
        pltpu.VMEM((2 * BAND, D), bf),
        pltpu.VMEM((OWN_N, D), f32),
        pltpu.SemaphoreType.DMA((3,)),
        pltpu.SemaphoreType.DMA((QUADS, 4, 3, 3)),
        pltpu.SemaphoreType.DMA((QUADS, 4, 3, 3)),
        pltpu.SemaphoreType.DMA((8,)),
        pltpu.SemaphoreType.DMA((8,)),
        pltpu.SemaphoreType.DMA((8,)),
        pltpu.SemaphoreType.DMA((8,)),
    ]
    vmem = pl.BlockSpec(memory_space=pltpu.VMEM)
    anywhere = pl.BlockSpec(memory_space=pl.ANY)
    return pl.pallas_call(
        functools.partial(fused_kernel, scale),
        out_shape=[
            jax.ShapeDtypeStruct((OWN_N, D), bf),
            jax.ShapeDtypeStruct((8, 3 * D), f32),
        ],
        in_specs=[vmem, vmem, anywhere, anywhere, anywhere],
        out_specs=[vmem, vmem],
        scratch_shapes=scratch,
        compiler_params=pltpu.CompilerParams(
            collective_id=0, has_side_effects=True, vmem_limit_bytes=61 * 2**20
        ),
        name="attention_backward",
    )(x, pack, go, w, side)


def body(inputs, grad_out, w_qkv):
    scale = float(2 * 128 * 256) ** -0.5
    gi, gw = fused(inputs.reshape(OWN_N, D), grad_out.reshape(OWN_N, D), w_qkv, scale)
    return gi.reshape(inputs.shape), gw


def solution(mesh):
    in_specs = (P("dp", "lat", "lon", None), P("dp", "lat", "lon", None), P())
    out_specs = (P("dp", "lat", "lon", None), P(("dp", "lat", "lon"), None))
    return jax.shard_map(body, mesh=mesh, in_specs=in_specs, out_specs=out_specs, check_vma=False)
```

```python
import functools

import jax
import jax.numpy as jnp
import numpy as np
from jax import lax
from jax.experimental import pallas as pl
from jax.experimental.pallas import tpu as pltpu
from jax.sharding import PartitionSpec as P

WIN = 13
MARGIN = WIN // 2
HEAD = 64
QUAD = 4
WIDTH = QUAD * HEAD
LAT_DEV = 32
LON_DEV = 16
ROW_T = 4
TILES = LAT_DEV // ROW_T
QUERIES = ROW_T * LON_DEV
KEY_ROWS = ROW_T + WIN - 1
SIDE = 2 * MARGIN
KEYS_A = KEY_ROWS * LON_DEV
KEYS_B = KEY_ROWS * SIDE
KEYS = KEYS_A + KEYS_B
PAD_ROWS = 2
OWN = (PAD_ROWS + MARGIN) * LON_DEV
OWN_N = LAT_DEV * LON_DEV
SPLIT = (PAD_ROWS + LAT_DEV + SIDE) * LON_DEV
TOKENS = 1280
D = 1024
NT = (((1,), (1,)), ((), ()))
TN = (((0,), (0,)), ((), ()))
NN = (((1,), (0,)), ((), ()))
MESH = pl.DeviceIdType.MESH


def mm(a, b, dims=NN):
    return lax.dot_general(a, b, dims, preferred_element_type=jnp.float32)


def key_tile(t, first_band, last_band):
    lead = jnp.logical_and(first_band, t == 0).astype(jnp.int32)
    tail = jnp.logical_and(last_band, t == TILES - 1).astype(jnp.int32)
    return t + lead - tail


def window_bias(t, top, keys, side, band_start, total_rows):
    kk = lax.broadcasted_iota(jnp.int32, (keys, WIDTH), 0)
    qq = lax.broadcasted_iota(jnp.int32, (keys, WIDTH), 1) & (QUERIES - 1)
    i, j = qq >> 4, qq & 15
    if side:
        r = (kk * 171) >> 11
        c = kk - r * SIDE
        col = jnp.where(c < MARGIN, c - MARGIN, c + (LON_DEV - MARGIN))
    else:
        r, col = kk >> 4, kk & 15
    first = band_start + ROW_T * t
    key_row = band_start + ROW_T * top - MARGIN + r
    start = jnp.clip(first + i - MARGIN, 0, total_rows - WIN)
    off = key_row - start
    away = col - j
    inside = (off >= 0) & (off < WIN) & (away >= -MARGIN) & (away <= MARGIN)
    return jnp.where(inside, 0.0, -1e30).astype(jnp.float32)


def spread(tile, same_head):
    return jnp.concatenate([tile] * QUAD, axis=0) * same_head


def attend(t, top, cols, q, kv, vv, go, bias, same, dk, dv, dq):
    own = pl.ds(t * QUERIES, QUERIES)
    ka = pl.ds(pl.multiple_of(PAD_ROWS * LON_DEV + top * QUERIES, 32), KEYS_A)
    kb = pl.ds(pl.multiple_of(SPLIT + top * ROW_T * SIDE, 16), KEYS_B)
    kind = min(t, 2) if t < TILES - 2 else t - TILES + 5
    same_head = same[...]
    bq = spread(q[own, cols], same_head)
    bg = spread(go[own, cols], same_head)
    keys_a, keys_b = kv[ka, cols], kv[kb, cols]
    sa = mm(keys_a, bq, NT) + bias[kind, :KEYS_A, :]
    sb = mm(keys_b, bq, NT) + bias[kind, KEYS_A:, :]
    peak = jnp.maximum(jnp.max(sa, axis=0, keepdims=True), jnp.max(sb, axis=0, keepdims=True))
    pa = jnp.exp(sa - peak)
    pb = jnp.exp(sb - peak)
    da = mm(vv[ka, cols], bg, NT)
    db = mm(vv[kb, cols], bg, NT)
    inv = 1.0 / (jnp.sum(pa, axis=0, keepdims=True) + jnp.sum(pb, axis=0, keepdims=True))
    delta = (
        jnp.sum(pa * da, axis=0, keepdims=True) + jnp.sum(pb * db, axis=0, keepdims=True)
    ) * inv
    pa = pa * inv
    pb = pb * inv
    aa = pa.astype(jnp.bfloat16)
    ab = pb.astype(jnp.bfloat16)
    ea = (pa * (da - delta)).astype(jnp.bfloat16)
    eb = (pb * (db - delta)).astype(jnp.bfloat16)
    dk[ka, :] += mm(ea, bq)
    dk[kb, :] += mm(eb, bq)
    dv[ka, :] += mm(aa, bg)
    dv[kb, :] += mm(ab, bg)
    mixed = (mm(ea, keys_a, TN) + mm(eb, keys_b, TN)) * same_head.astype(jnp.float32)
    total = mixed[:QUERIES]
    for h in range(1, QUAD):
        total = total + mixed[h * QUERIES : (h + 1) * QUERIES]
    rows = pl.ds(OWN + t * QUERIES, QUERIES)
    dq[rows, cols] = (total * HEAD**-0.5).astype(jnp.bfloat16)


STAGES = (2, 4, 4, 4)
LEFT = (512, 128, 32, 8)


def place():
    lon = lax.axis_index("lon")
    return lax.axis_index("dp"), lax.axis_index("lat"), lon >> 3, (lon >> 1) & 3, lon & 1


def device(xlo, y, xhi, z, core):
    return (xlo, y, xhi * 8 + z * 2 + core)


ORDERS = ("zyx", "yxz", "xzy")


def along(axis):
    xlo, y, xhi, z, core = place()
    me = {"x": xhi * 2 + xlo, "y": y, "z": z}[axis]
    others = []
    for step in (1, 3, 2):
        to = (me + step) & 3
        if axis == "z":
            others.append((to, device(xlo, y, xhi, to, core)))
        elif axis == "y":
            others.append((to, device(xlo, to, xhi, z, core)))
        else:
            others.append((to, device(to & 1, y, to >> 1, z, core)))
    return me, others


def peers(stage, i):
    if stage == 0:
        xlo, y, xhi, z, core = place()
        return core, [(1 - core, device(xlo, y, xhi, z, 1 - core))]
    return along(ORDERS[i][stage - 1])


def by_owner(value, order):
    blocks = []
    for core in range(2):
        for n in range(64):
            at = dict(zip(order, (n >> 4, (n >> 2) & 3, n & 3)))
            xlo, xhi = at["x"] & 1, at["x"] >> 1
            start = ((((xlo * 4 + at["y"]) * 2 + xhi) * 4 + at["z"]) * 2 + core) * 8
            blocks.append(value[start : start + 8])
    return jnp.concatenate(blocks, axis=0)


SLOTS = ((0, 192, 0, -1), (192, 192, 0, 1), (384, 48, -1, -1), (432, 48, -1, 1), (480, 48, 1, -1), (528, 48, 1, 1))
OPPOSITE = (1, 0, 5, 4, 3, 2)
PACKED = 576
SIDES = TOKENS - SPLIT
ABOVE = PAD_ROWS * LON_DEV
BELOW = OWN + OWN_N
BAND = MARGIN * LON_DEV
QUADS = D // WIDTH


def packing():
    pack = np.zeros((PACKED, OWN_N), np.float32)
    side = np.zeros((SIDES, PACKED), np.float32)
    for start, size, dy, dx in SLOTS:
        count = LAT_DEV if dy == 0 else MARGIN
        for r in range(count):
            for c in range(MARGIN):
                row = r + (LAT_DEV - MARGIN if dy > 0 else 0)
                col = c + (LON_DEV - MARGIN if dx > 0 else 0)
                pack[start + r * MARGIN + c, row * LON_DEV + col] = 1
                row = r + (MARGIN if dy == 0 else 0 if dy < 0 else LAT_DEV + MARGIN)
                col = c + (MARGIN if dx > 0 else 0)
                side[row * SIDE + col, start + r * MARGIN + c] = 1
    return [jnp.asarray(m, jnp.bfloat16) for m in (pack, side, pack.T, side.T)]


def fused_kernel(
    scale, x, pack, go_hbm, w_hbm, side_hbm, unpack_hbm, unside_hbm, gi, gw,
    go, w, side, unpack, unside, xe, packed, halo, q, k, v, dall, dk, dv, bias, same, xt,
    part, held1, held2, held3, got0, got1, got2, got3,
    back, lat_out, lat_in, own_grad,
    load, send, recv, halo_send, halo_recv, back_send, back_recv,
):
    dp, lat, lon = lax.axis_index("dp"), lax.axis_index("lat"), lax.axis_index("lon")
    lats, lons = lax.axis_size("lat"), lax.axis_size("lon")
    band_start = lat * LAT_DEV
    total_rows = LAT_DEV * lats
    first_band, last_band = lat == 0, lat == lats - 1
    held = (part, held1, held2, held3)
    got = (got0, got1, got2, got3)

    loads = [
        pltpu.make_async_copy(w_hbm, w, load.at[0]),
        pltpu.make_async_copy(go_hbm, go, load.at[1]),
        pltpu.make_async_copy(side_hbm, side, load.at[2]),
        pltpu.make_async_copy(unpack_hbm, unpack, load.at[3]),
        pltpu.make_async_copy(unside_hbm, unside, load.at[4]),
    ]
    for copy in loads:
        copy.start()

    def when_there(dy, act):
        if dy == 0:
            act()
        else:
            pl.when(lat > 0 if dy < 0 else lat < lats - 1)(act)

    def neighbour(dy, dx):
        return (dp, lat + dy, lax.rem(lon + dx + lons, lons))

    moves = [(dy, dx) for _, _, dy, dx in SLOTS] + [(-1, 0), (1, 0)]

    packed[...] = mm(pack[...], x[...]).astype(jnp.bfloat16)

    barrier = pltpu.get_barrier_semaphore()
    count = 0
    for others in (peers(0, 0)[1], along("x")[1], along("y")[1], along("z")[1]):
        for _, dev in others:
            pl.semaphore_signal(barrier, inc=1, device_id=dev, device_id_type=MESH)
            count += 1
    for dy, dx in moves:
        @functools.partial(when_there, dy)
        def _():
            pl.semaphore_signal(barrier, inc=1, device_id=neighbour(dy, dx), device_id_type=MESH)
    count = count + 2 + 3 * (lat > 0).astype(jnp.int32) + 3 * (lat < lats - 1).astype(jnp.int32)
    pl.semaphore_wait(barrier, count)

    def exchange(source, target, up, down, into_up, into_down, sends, recvs, sending):
        for n, (dy, dx) in enumerate(moves):
            @functools.partial(when_there, dy)
            def _():
                if n < 6:
                    other = OPPOSITE[n]
                    start, size = SLOTS[n][:2]
                    there = SLOTS[other][0]
                    src = source.at[pl.ds(start, size), :]
                    far, near = target.at[pl.ds(there, size), :], target.at[pl.ds(start, size), :]
                else:
                    other = 13 - n
                    src = (up, down)[n - 6]
                    far, near = (into_down, into_up) if n == 6 else (into_up, into_down)
                copy = pltpu.make_async_remote_copy(
                    src_ref=src,
                    dst_ref=far if sending else near,
                    send_sem=sends.at[n],
                    recv_sem=recvs.at[other if sending else n],
                    device_id=neighbour(dy, dx),
                    device_id_type=MESH,
                )
                if sending:
                    copy.start()
                else:
                    copy.wait()

    def halo_exchange(sending):
        exchange(
            packed, halo, x.at[pl.ds(0, BAND), :], x.at[pl.ds(OWN_N - BAND, BAND), :],
            xe.at[pl.ds(ABOVE, BAND), :], xe.at[pl.ds(BELOW, BAND), :],
            halo_send, halo_recv, sending,
        )

    def give_back(sending):
        exchange(
            packed, back, lat_out.at[pl.ds(0, BAND), :], lat_out.at[pl.ds(BAND, BAND), :],
            lat_in.at[pl.ds(0, BAND), :], lat_in.at[pl.ds(BAND, BAND), :],
            back_send, back_recv, sending,
        )

    halo_exchange(True)

    for there, slot in ((lat > 0, 384), (lat < lats - 1, 480)):
        @pl.when(jnp.logical_not(there))
        def _():
            zero = jnp.zeros((96, D), jnp.bfloat16)
            halo[slot : slot + 96, :] = zero
            back[slot : slot + 96, :] = zero
            at = ABOVE if slot == 384 else BELOW
            xe[at : at + BAND, :] = zero
            at = 0 if slot == 384 else BAND
            lat_in[at : at + BAND, :] = zero

    xe[:ABOVE, :] = jnp.zeros((ABOVE, D), jnp.bfloat16)
    xe[OWN : OWN + OWN_N, :] = x[...]
    row = lax.broadcasted_iota(jnp.int32, (WIDTH, WIDTH), 0)
    col = lax.broadcasted_iota(jnp.int32, (WIDTH, WIDTH), 1)
    same[...] = jnp.where((row >> 6) == (col >> 6), 1.0, 0.0).astype(jnp.bfloat16)

    loads[0].wait()

    @pl.loop(0, QUADS)
    def _(b):
        cols = pl.ds(pl.multiple_of(b * WIDTH, WIDTH), WIDTH)
        kcols = pl.ds(pl.multiple_of(D + b * WIDTH, WIDTH), WIDTH)
        vcols = pl.ds(pl.multiple_of(2 * D + b * WIDTH, WIDTH), WIDTH)
        q[:, cols] = mm(x[...], w[:, cols]).astype(jnp.bfloat16) * jnp.bfloat16(0.125)
        k[OWN : OWN + OWN_N, cols] = mm(x[...], w[:, kcols]).astype(jnp.bfloat16)
        v[OWN : OWN + OWN_N, cols] = mm(x[...], w[:, vcols]).astype(jnp.bfloat16)

    @pl.loop(0, 5)
    def _(n):
        t = n + (TILES - 5) * (n >= 3).astype(jnp.int32)
        top = key_tile(t, first_band, last_band)
        bias[n, :KEYS_A, :] = window_bias(t, top, KEYS_A, False, band_start, total_rows)
        bias[n, KEYS_A:, :] = window_bias(t, top, KEYS_B, True, band_start, total_rows)

    for copy in loads[1:]:
        copy.wait()
    halo_exchange(False)
    xe[SPLIT:, :] = mm(side[...], halo[...]).astype(jnp.bfloat16)

    @pl.loop(0, QUADS)
    def _(b):
        cols = pl.ds(pl.multiple_of(b * WIDTH, WIDTH), WIDTH)
        kcols = pl.ds(pl.multiple_of(D + b * WIDTH, WIDTH), WIDTH)
        vcols = pl.ds(pl.multiple_of(2 * D + b * WIDTH, WIDTH), WIDTH)
        outer = jnp.concatenate([xe[:OWN, :], xe[BELOW:, :]], axis=0)
        for into, wcols in ((k, kcols), (v, vcols)):
            value = mm(outer, w[:, wcols]).astype(jnp.bfloat16)
            into[:OWN, cols] = value[:OWN]
            into[BELOW:, cols] = value[OWN:]
        rows = pl.ds(pl.multiple_of(b * 256, 256), 256)
        xt[rows, :] = xe[:, rows].T

    def copies(c, stage, i):
        return [
            pltpu.make_async_remote_copy(
                src_ref=held[stage].at[c, i, pl.ds(to * LEFT[stage], LEFT[stage]), :],
                dst_ref=got[stage].at[c, i, n],
                send_sem=send.at[c, stage, i, n],
                recv_sem=recv.at[c, stage, i, n],
                device_id=dev,
                device_id_type=MESH,
            )
            for n, (to, dev) in enumerate(peers(stage, i)[1])
        ]

    def begin(c, stage, i):
        for copy in copies(c, stage, i):
            copy.start()

    def finish(c, stage):
        for i in range(3):
            for copy in copies(c, stage, i):
                copy.wait()
            me, others = peers(stage, i)
            rows = pl.ds(pl.multiple_of(me * LEFT[stage], LEFT[stage]), LEFT[stage])
            value = held[stage][c, i, rows, :].astype(jnp.float32)
            for n in range(len(others)):
                value = value + got[stage][c, i, n].astype(jnp.float32)
            if stage == 3:
                at = i * D + c * WIDTH
                at = at if isinstance(at, int) else pl.multiple_of(at, WIDTH)
                gw[:, pl.ds(at, WIDTH)] = value
            else:
                held[stage + 1][c, i] = value.astype(held[stage + 1].dtype)
                begin(c, stage + 1, i)

    @pl.loop(0, QUADS)
    def _(g):
        cols = pl.ds(pl.multiple_of(g * WIDTH, WIDTH), WIDTH)
        kcols = pl.ds(pl.multiple_of(D + g * WIDTH, WIDTH), WIDTH)
        vcols = pl.ds(pl.multiple_of(2 * D + g * WIDTH, WIDTH), WIDTH)
        dk[...] = jnp.zeros_like(dk)
        dv[...] = jnp.zeros_like(dv)

        def tiles(a, b):
            for t in range(a, b):
                top = key_tile(t, first_band, last_band)
                attend(t, top, cols, q, k, v, go, bias, same, dk, dv, dall)

        tiles(0, 5)

        @pl.when(g >= 1)
        def _():
            finish(g - 1, 0)

        tiles(5, TILES)

        @pl.when(g >= 2)
        def _():
            finish(g - 2, 2)

        dall[:, kcols] = dk[...].astype(jnp.bfloat16)
        dall[:, vcols] = dv[...].astype(jnp.bfloat16)
        mine = pl.ds(OWN, OWN_N)
        for i, tokens, wide in ((0, mine, cols), (1, slice(None), kcols), (2, slice(None), vcols)):
            value = mm(xt[:, tokens], dall[tokens, wide]) * scale
            part[g, i] = by_owner(value, ORDERS[i]).astype(jnp.bfloat16)
            begin(g, 0, i)

        @pl.when(g >= 1)
        def _():
            finish(g - 1, 1)

        @pl.when(g >= 2)
        def _():
            finish(g - 2, 3)

    def edge_grads(b):
        cols = pl.ds(b * WIDTH, WIDTH)
        rows = jnp.concatenate([dall[ABOVE:OWN, D:], dall[BELOW:, D:]], axis=0)
        value = mm(rows, w[cols, D:], NT).astype(jnp.bfloat16)
        lat_out[:, cols] = value[: 2 * BAND]
        packed[:, cols] = mm(unside[...], value[2 * BAND :]).astype(jnp.bfloat16)

    def own_grads(b):
        cols = pl.ds(b * WIDTH, WIDTH)
        own_grad[:, cols] = mm(dall[OWN:BELOW, :], w[cols, :], NT)

    edge_grads(0)
    edge_grads(1)
    finish(3, 0)
    finish(2, 2)
    edge_grads(2)
    edge_grads(3)
    give_back(True)
    finish(3, 1)
    own_grads(0)
    own_grads(1)
    finish(3, 2)
    own_grads(2)
    own_grads(3)
    finish(2, 3)
    give_back(False)

    for b in range(QUADS):
        cols = pl.ds(b * WIDTH, WIDTH)
        value = own_grad[:, cols] + mm(unpack[...], back[:, cols])
        gi[BAND : OWN_N - BAND, cols] = value[BAND : OWN_N - BAND].astype(jnp.bfloat16)
        gi[:BAND, cols] = (value[:BAND] + lat_in[:BAND, cols].astype(jnp.float32)).astype(jnp.bfloat16)
        gi[OWN_N - BAND :, cols] = (
            value[OWN_N - BAND :] + lat_in[BAND:, cols].astype(jnp.float32)
        ).astype(jnp.bfloat16)

    finish(3, 3)


def copy_kernel(gi_in, gw_in, gi, gw):
    gi[...] = gi_in[...]
    gw[...] = gw_in[...]


def handed_over(gi, gw):
    vmem = pl.BlockSpec(memory_space=pltpu.VMEM)
    return pl.pallas_call(
        copy_kernel,
        out_shape=[jax.ShapeDtypeStruct(t.shape, t.dtype) for t in (gi, gw)],
        in_specs=[vmem] * 2,
        out_specs=[vmem] * 2,
        name="hand_over",
    )(gi, gw)


def fused(x, go, w, scale):
    bf, f32 = jnp.bfloat16, jnp.float32
    kinds = (bf, bf, bf, f32)
    pack, side, unpack, unside = packing()
    scratch = [
        pltpu.VMEM((OWN_N, D), bf),
        pltpu.VMEM((D, 3 * D), bf),
        pltpu.VMEM((SIDES, PACKED), bf),
        pltpu.VMEM((OWN_N, PACKED), bf),
        pltpu.VMEM((PACKED, SIDES), bf),
        pltpu.VMEM((TOKENS, D), bf),
        pltpu.VMEM((PACKED, D), bf),
        pltpu.VMEM((PACKED, D), bf),
        pltpu.VMEM((OWN_N, D), bf),
        pltpu.VMEM((TOKENS, D), bf),
        pltpu.VMEM((TOKENS, D), bf),
        pltpu.VMEM((TOKENS, 3 * D), bf),
        pltpu.VMEM((TOKENS, WIDTH), f32),
        pltpu.VMEM((TOKENS, WIDTH), f32),
        pltpu.VMEM((5, KEYS, WIDTH), f32),
        pltpu.VMEM((WIDTH, WIDTH), bf),
        pltpu.VMEM((D, TOKENS), bf),
        pltpu.VMEM((QUADS, 3, D, WIDTH), bf),
    ]
    scratch += [pltpu.VMEM((QUADS, 3, LEFT[s - 1], WIDTH), kinds[s]) for s in range(1, 4)]
    scratch += [pltpu.VMEM((QUADS, 3, STAGES[s] - 1, LEFT[s], WIDTH), kinds[s]) for s in range(4)]
    scratch += [
        pltpu.VMEM((PACKED, D), bf),
        pltpu.VMEM((2 * BAND, D), bf),
        pltpu.VMEM((2 * BAND, D), bf),
        pltpu.VMEM((OWN_N, D), f32),
        pltpu.SemaphoreType.DMA((5,)),
        pltpu.SemaphoreType.DMA((QUADS, 4, 3, 3)),
        pltpu.SemaphoreType.DMA((QUADS, 4, 3, 3)),
        pltpu.SemaphoreType.DMA((8,)),
        pltpu.SemaphoreType.DMA((8,)),
        pltpu.SemaphoreType.DMA((8,)),
        pltpu.SemaphoreType.DMA((8,)),
    ]
    vmem = pl.BlockSpec(memory_space=pltpu.VMEM)
    anywhere = pl.BlockSpec(memory_space=pl.ANY)
    return pl.pallas_call(
        functools.partial(fused_kernel, scale),
        out_shape=[
            jax.ShapeDtypeStruct((OWN_N, D), bf),
            jax.ShapeDtypeStruct((8, 3 * D), f32),
        ],
        in_specs=[vmem, vmem] + [anywhere] * 5,
        out_specs=[vmem, vmem],
        scratch_shapes=scratch,
        compiler_params=pltpu.CompilerParams(
            collective_id=0, has_side_effects=True, vmem_limit_bytes=61 * 2**20
        ),
        name="attention_backward",
    )(x, pack, go, w, side, unpack, unside)


def body(inputs, grad_out, w_qkv):
    scale = float(2 * 128 * 256) ** -0.5
    gi, gw = fused(inputs.reshape(OWN_N, D), grad_out.reshape(OWN_N, D), w_qkv, scale)
    gi, gw = handed_over(gi, gw)
    return gi.reshape(inputs.shape), gw


def solution(mesh):
    in_specs = (P("dp", "lat", "lon", None), P("dp", "lat", "lon", None), P())
    out_specs = (P("dp", "lat", "lon", None), P(("dp", "lat", "lon"), None))
    return jax.shard_map(body, mesh=mesh, in_specs=in_specs, out_specs=out_specs, check_vma=False)
```

```python
import functools

import jax
import jax.numpy as jnp
import numpy as np
from jax import lax
from jax.experimental import pallas as pl
from jax.experimental.pallas import tpu as pltpu
from jax.sharding import PartitionSpec as P

WIN = 13
MARGIN = WIN // 2
HEAD = 64
QUAD = 4
WIDTH = QUAD * HEAD
LAT_DEV = 32
LON_DEV = 16
ROW_T = 4
TILES = LAT_DEV // ROW_T
QUERIES = ROW_T * LON_DEV
KEY_ROWS = ROW_T + WIN - 1
SIDE = 2 * MARGIN
KEYS_A = KEY_ROWS * LON_DEV
KEYS_B = KEY_ROWS * SIDE
KEYS = KEYS_A + KEYS_B
PAD_ROWS = 2
OWN = (PAD_ROWS + MARGIN) * LON_DEV
OWN_N = LAT_DEV * LON_DEV
SPLIT = (PAD_ROWS + LAT_DEV + SIDE) * LON_DEV
TOKENS = 1280
D = 1024
NT = (((1,), (1,)), ((), ()))
TN = (((0,), (0,)), ((), ()))
NN = (((1,), (0,)), ((), ()))
MESH = pl.DeviceIdType.MESH


def mm(a, b, dims=NN):
    return lax.dot_general(a, b, dims, preferred_element_type=jnp.float32)


def key_tile(t, first_band, last_band):
    lead = jnp.logical_and(first_band, t == 0).astype(jnp.int32)
    tail = jnp.logical_and(last_band, t == TILES - 1).astype(jnp.int32)
    return t + lead - tail


def window_bias(t, top, keys, side, band_start, total_rows):
    kk = lax.broadcasted_iota(jnp.int32, (keys, WIDTH), 0)
    qq = lax.broadcasted_iota(jnp.int32, (keys, WIDTH), 1) & (QUERIES - 1)
    i, j = qq >> 4, qq & 15
    if side:
        r = (kk * 171) >> 11
        c = kk - r * SIDE
        col = jnp.where(c < MARGIN, c - MARGIN, c + (LON_DEV - MARGIN))
    else:
        r, col = kk >> 4, kk & 15
    first = band_start + ROW_T * t
    key_row = band_start + ROW_T * top - MARGIN + r
    start = jnp.clip(first + i - MARGIN, 0, total_rows - WIN)
    off = key_row - start
    away = col - j
    inside = (off >= 0) & (off < WIN) & (away >= -MARGIN) & (away <= MARGIN)
    return jnp.where(inside, 0.0, -1e30).astype(jnp.float32)


def spread(tile, same_head):
    return jnp.concatenate([tile] * QUAD, axis=0) * same_head


def attend(t, top, cols, q, kv, vv, go, bias, same, dk, dv, dq):
    own = pl.ds(t * QUERIES, QUERIES)
    ka = pl.ds(pl.multiple_of(PAD_ROWS * LON_DEV + top * QUERIES, 32), KEYS_A)
    kb = pl.ds(pl.multiple_of(SPLIT + top * ROW_T * SIDE, 16), KEYS_B)
    kind = min(t, 2) if t < TILES - 2 else t - TILES + 5
    same_head = same[...]
    bq = spread(q[own, cols], same_head)
    bg = spread(go[own, cols], same_head)
    keys_a, keys_b = kv[ka, cols], kv[kb, cols]
    sa = mm(keys_a, bq, NT) + bias[kind, :KEYS_A, :]
    sb = mm(keys_b, bq, NT) + bias[kind, KEYS_A:, :]
    peak = jnp.maximum(jnp.max(sa, axis=0, keepdims=True), jnp.max(sb, axis=0, keepdims=True))
    pa = jnp.exp(sa - peak)
    pb = jnp.exp(sb - peak)
    da = mm(vv[ka, cols], bg, NT)
    db = mm(vv[kb, cols], bg, NT)
    inv = 1.0 / (jnp.sum(pa, axis=0, keepdims=True) + jnp.sum(pb, axis=0, keepdims=True))
    delta = (
        jnp.sum(pa * da, axis=0, keepdims=True) + jnp.sum(pb * db, axis=0, keepdims=True)
    ) * inv
    pa = pa * inv
    pb = pb * inv
    aa = pa.astype(jnp.bfloat16)
    ab = pb.astype(jnp.bfloat16)
    ea = (pa * (da - delta)).astype(jnp.bfloat16)
    eb = (pb * (db - delta)).astype(jnp.bfloat16)
    dk[ka, :] += mm(ea, bq)
    dk[kb, :] += mm(eb, bq)
    dv[ka, :] += mm(aa, bg)
    dv[kb, :] += mm(ab, bg)
    mixed = (mm(ea, keys_a, TN) + mm(eb, keys_b, TN)) * same_head.astype(jnp.float32)
    total = mixed[:QUERIES]
    for h in range(1, QUAD):
        total = total + mixed[h * QUERIES : (h + 1) * QUERIES]
    rows = pl.ds(OWN + t * QUERIES, QUERIES)
    dq[rows, cols] = (total * HEAD**-0.5).astype(jnp.bfloat16)


STAGES = (2, 4, 4, 4)
LEFT = (512, 128, 32, 8)


def place():
    lon = lax.axis_index("lon")
    return lax.axis_index("dp"), lax.axis_index("lat"), lon >> 3, (lon >> 1) & 3, lon & 1


def device(xlo, y, xhi, z, core):
    return (xlo, y, xhi * 8 + z * 2 + core)


ORDERS = ("zyx", "yxz", "xzy")


def along(axis):
    xlo, y, xhi, z, core = place()
    me = {"x": xhi * 2 + xlo, "y": y, "z": z}[axis]
    others = []
    for step in (1, 3, 2):
        to = (me + step) & 3
        if axis == "z":
            others.append((to, device(xlo, y, xhi, to, core)))
        elif axis == "y":
            others.append((to, device(xlo, to, xhi, z, core)))
        else:
            others.append((to, device(to & 1, y, to >> 1, z, core)))
    return me, others


def peers(stage, i):
    if stage == 0:
        xlo, y, xhi, z, core = place()
        return core, [(1 - core, device(xlo, y, xhi, z, 1 - core))]
    return along(ORDERS[i][stage - 1])


def by_owner(value, order):
    blocks = []
    for core in range(2):
        for n in range(64):
            at = dict(zip(order, (n >> 4, (n >> 2) & 3, n & 3)))
            xlo, xhi = at["x"] & 1, at["x"] >> 1
            start = ((((xlo * 4 + at["y"]) * 2 + xhi) * 4 + at["z"]) * 2 + core) * 8
            blocks.append(value[start : start + 8])
    return jnp.concatenate(blocks, axis=0)


SLOTS = ((0, 192, 0, -1), (192, 192, 0, 1), (384, 48, -1, -1), (432, 48, -1, 1), (480, 48, 1, -1), (528, 48, 1, 1))
OPPOSITE = (1, 0, 5, 4, 3, 2)
PACKED = 576
SIDES = TOKENS - SPLIT
ABOVE = PAD_ROWS * LON_DEV
BELOW = OWN + OWN_N
BAND = MARGIN * LON_DEV
QUADS = D // WIDTH


def packing():
    pack = np.zeros((PACKED, OWN_N), np.float32)
    side = np.zeros((SIDES, PACKED), np.float32)
    for start, size, dy, dx in SLOTS:
        count = LAT_DEV if dy == 0 else MARGIN
        for r in range(count):
            for c in range(MARGIN):
                row = r + (LAT_DEV - MARGIN if dy > 0 else 0)
                col = c + (LON_DEV - MARGIN if dx > 0 else 0)
                pack[start + r * MARGIN + c, row * LON_DEV + col] = 1
                row = r + (MARGIN if dy == 0 else 0 if dy < 0 else LAT_DEV + MARGIN)
                col = c + (MARGIN if dx > 0 else 0)
                side[row * SIDE + col, start + r * MARGIN + c] = 1
    return [jnp.asarray(m, jnp.bfloat16) for m in (pack, side, pack.T, side.T)]


def fused_kernel(
    scale, x, pack, go_hbm, w_hbm, side_hbm, unpack_hbm, unside_hbm, gi, gw,
    go, w, side, unpack, unside, xe, packed, halo, q, k, v, dall, dk, dv, bias, same, xt,
    part, held1, held2, held3, got0, got1, got2, got3,
    back, lat_out, lat_in, own_grad, early,
    load, send, recv, halo_send, halo_recv, back_send, back_recv,
):
    dp, lat, lon = lax.axis_index("dp"), lax.axis_index("lat"), lax.axis_index("lon")
    lats, lons = lax.axis_size("lat"), lax.axis_size("lon")
    band_start = lat * LAT_DEV
    total_rows = LAT_DEV * lats
    first_band, last_band = lat == 0, lat == lats - 1
    held = (part, held1, held2, held3)
    got = (got0, got1, got2, got3)

    loads = [
        pltpu.make_async_copy(w_hbm, w, load.at[0]),
        pltpu.make_async_copy(go_hbm, go, load.at[1]),
        pltpu.make_async_copy(side_hbm, side, load.at[2]),
        pltpu.make_async_copy(unpack_hbm, unpack, load.at[3]),
        pltpu.make_async_copy(unside_hbm, unside, load.at[4]),
    ]
    for copy in loads:
        copy.start()

    def when_there(dy, act):
        if dy == 0:
            act()
        else:
            pl.when(lat > 0 if dy < 0 else lat < lats - 1)(act)

    def neighbour(dy, dx):
        return (dp, lat + dy, lax.rem(lon + dx + lons, lons))

    moves = [(dy, dx) for _, _, dy, dx in SLOTS] + [(-1, 0), (1, 0)]

    packed[...] = mm(pack[...], x[...]).astype(jnp.bfloat16)

    barrier = pltpu.get_barrier_semaphore()
    count = 0
    for others in (peers(0, 0)[1], along("x")[1], along("y")[1], along("z")[1]):
        for _, dev in others:
            pl.semaphore_signal(barrier, inc=1, device_id=dev, device_id_type=MESH)
            count += 1
    for dy, dx in moves:
        @functools.partial(when_there, dy)
        def _():
            pl.semaphore_signal(barrier, inc=1, device_id=neighbour(dy, dx), device_id_type=MESH)
    count = count + 2 + 3 * (lat > 0).astype(jnp.int32) + 3 * (lat < lats - 1).astype(jnp.int32)
    pl.semaphore_wait(barrier, count)

    def exchange(source, target, up, down, into_up, into_down, sends, recvs, sending):
        for n, (dy, dx) in enumerate(moves):
            @functools.partial(when_there, dy)
            def _():
                if n < 6:
                    other = OPPOSITE[n]
                    start, size = SLOTS[n][:2]
                    there = SLOTS[other][0]
                    src = source.at[pl.ds(start, size), :]
                    far, near = target.at[pl.ds(there, size), :], target.at[pl.ds(start, size), :]
                else:
                    other = 13 - n
                    src = (up, down)[n - 6]
                    far, near = (into_down, into_up) if n == 6 else (into_up, into_down)
                copy = pltpu.make_async_remote_copy(
                    src_ref=src,
                    dst_ref=far if sending else near,
                    send_sem=sends.at[n],
                    recv_sem=recvs.at[other if sending else n],
                    device_id=neighbour(dy, dx),
                    device_id_type=MESH,
                )
                if sending:
                    copy.start()
                else:
                    copy.wait()

    def halo_exchange(sending):
        exchange(
            packed, halo, x.at[pl.ds(0, BAND), :], x.at[pl.ds(OWN_N - BAND, BAND), :],
            xe.at[pl.ds(ABOVE, BAND), :], xe.at[pl.ds(BELOW, BAND), :],
            halo_send, halo_recv, sending,
        )

    def give_back(sending):
        exchange(
            packed, back, lat_out.at[pl.ds(0, BAND), :], lat_out.at[pl.ds(BAND, BAND), :],
            lat_in.at[pl.ds(0, BAND), :], lat_in.at[pl.ds(BAND, BAND), :],
            back_send, back_recv, sending,
        )

    halo_exchange(True)

    for there, slot in ((lat > 0, 384), (lat < lats - 1, 480)):
        @pl.when(jnp.logical_not(there))
        def _():
            zero = jnp.zeros((96, D), jnp.bfloat16)
            halo[slot : slot + 96, :] = zero
            back[slot : slot + 96, :] = zero
            at = ABOVE if slot == 384 else BELOW
            xe[at : at + BAND, :] = zero
            at = 0 if slot == 384 else BAND
            lat_in[at : at + BAND, :] = zero

    xe[:ABOVE, :] = jnp.zeros((ABOVE, D), jnp.bfloat16)
    xe[OWN : OWN + OWN_N, :] = x[...]
    row = lax.broadcasted_iota(jnp.int32, (WIDTH, WIDTH), 0)
    col = lax.broadcasted_iota(jnp.int32, (WIDTH, WIDTH), 1)
    same[...] = jnp.where((row >> 6) == (col >> 6), 1.0, 0.0).astype(jnp.bfloat16)

    loads[0].wait()

    @pl.loop(0, QUADS)
    def _(b):
        cols = pl.ds(pl.multiple_of(b * WIDTH, WIDTH), WIDTH)
        kcols = pl.ds(pl.multiple_of(D + b * WIDTH, WIDTH), WIDTH)
        vcols = pl.ds(pl.multiple_of(2 * D + b * WIDTH, WIDTH), WIDTH)
        q[:, cols] = mm(x[...], w[:, cols]).astype(jnp.bfloat16) * jnp.bfloat16(0.125)
        k[OWN : OWN + OWN_N, cols] = mm(x[...], w[:, kcols]).astype(jnp.bfloat16)
        v[OWN : OWN + OWN_N, cols] = mm(x[...], w[:, vcols]).astype(jnp.bfloat16)

    @pl.loop(0, 5)
    def _(n):
        t = n + (TILES - 5) * (n >= 3).astype(jnp.int32)
        top = key_tile(t, first_band, last_band)
        bias[n, :KEYS_A, :] = window_bias(t, top, KEYS_A, False, band_start, total_rows)
        bias[n, KEYS_A:, :] = window_bias(t, top, KEYS_B, True, band_start, total_rows)

    for copy in loads[1:]:
        copy.wait()
    halo_exchange(False)
    xe[SPLIT:, :] = mm(side[...], halo[...]).astype(jnp.bfloat16)

    @pl.loop(0, QUADS)
    def _(b):
        cols = pl.ds(pl.multiple_of(b * WIDTH, WIDTH), WIDTH)
        kcols = pl.ds(pl.multiple_of(D + b * WIDTH, WIDTH), WIDTH)
        vcols = pl.ds(pl.multiple_of(2 * D + b * WIDTH, WIDTH), WIDTH)
        outer = jnp.concatenate([xe[:OWN, :], xe[BELOW:, :]], axis=0)
        for into, wcols in ((k, kcols), (v, vcols)):
            value = mm(outer, w[:, wcols]).astype(jnp.bfloat16)
            into[:OWN, cols] = value[:OWN]
            into[BELOW:, cols] = value[OWN:]
        rows = pl.ds(pl.multiple_of(b * 256, 256), 256)
        xt[rows, :] = xe[:, rows].T

    def copies(c, stage, i):
        return [
            pltpu.make_async_remote_copy(
                src_ref=held[stage].at[c, i, pl.ds(to * LEFT[stage], LEFT[stage]), :],
                dst_ref=got[stage].at[c, i, n],
                send_sem=send.at[c, stage, i, n],
                recv_sem=recv.at[c, stage, i, n],
                device_id=dev,
                device_id_type=MESH,
            )
            for n, (to, dev) in enumerate(peers(stage, i)[1])
        ]

    def begin(c, stage, i):
        for copy in copies(c, stage, i):
            copy.start()

    def finish(c, stage):
        for i in (2, 0, 1):
            for copy in copies(c, stage, i):
                copy.wait()
            me, others = peers(stage, i)
            rows = pl.ds(pl.multiple_of(me * LEFT[stage], LEFT[stage]), LEFT[stage])
            value = held[stage][c, i, rows, :].astype(jnp.float32)
            for n in range(len(others)):
                value = value + got[stage][c, i, n].astype(jnp.float32)
            if stage == 3:
                at = i * D + c * WIDTH
                at = at if isinstance(at, int) else pl.multiple_of(at, WIDTH)
                gw[:, pl.ds(at, WIDTH)] = value
            else:
                held[stage + 1][c, i] = value.astype(held[stage + 1].dtype)
                begin(c, stage + 1, i)

    def edges(a, b):
        return jnp.concatenate([dall[ABOVE:OWN, a:b], dall[BELOW:, a:b]], axis=0)

    @pl.loop(0, QUADS)
    def _(g):
        cols = pl.ds(pl.multiple_of(g * WIDTH, WIDTH), WIDTH)
        kcols = pl.ds(pl.multiple_of(D + g * WIDTH, WIDTH), WIDTH)
        vcols = pl.ds(pl.multiple_of(2 * D + g * WIDTH, WIDTH), WIDTH)
        dk[...] = jnp.zeros_like(dk)
        dv[...] = jnp.zeros_like(dv)

        def tiles(a, b):
            for t in range(a, b):
                top = key_tile(t, first_band, last_band)
                attend(t, top, cols, q, k, v, go, bias, same, dk, dv, dall)

        @pl.when(g == QUADS - 1)
        def _():
            @pl.loop(0, QUADS)
            def _(b):
                out = pl.ds(pl.multiple_of(b * WIDTH, WIDTH), WIDTH)
                early[:, out] = mm(edges(D, 2 * D - WIDTH), w[out, D : 2 * D - WIDTH], NT) + mm(
                    edges(2 * D, 3 * D - WIDTH), w[out, 2 * D : 3 * D - WIDTH], NT
                )

        tiles(0, 5)

        @pl.when(g >= 1)
        def _():
            finish(g - 1, 0)

        tiles(5, TILES)

        @pl.when(g >= 2)
        def _():
            finish(g - 2, 2)

        dall[:, kcols] = dk[...].astype(jnp.bfloat16)
        dall[:, vcols] = dv[...].astype(jnp.bfloat16)
        mine = pl.ds(OWN, OWN_N)
        for i, tokens, wide in ((0, mine, cols), (1, slice(None), kcols), (2, slice(None), vcols)):
            value = mm(xt[:, tokens], dall[tokens, wide]) * scale
            part[g, i] = by_owner(value, ORDERS[i]).astype(jnp.bfloat16)
            begin(g, 0, i)

        @pl.when(g >= 1)
        def _():
            finish(g - 1, 1)

        @pl.when(g >= 2)
        def _():
            finish(g - 2, 3)

    def edge_grads(b):
        cols = pl.ds(b * WIDTH, WIDTH)
        late = mm(edges(2 * D - WIDTH, 2 * D), w[cols, 2 * D - WIDTH : 2 * D], NT) + mm(
            edges(3 * D - WIDTH, 3 * D), w[cols, 3 * D - WIDTH :], NT
        )
        value = (early[:, cols] + late).astype(jnp.bfloat16)
        lat_out[:, cols] = value[: 2 * BAND]
        packed[:, cols] = mm(unside[...], value[2 * BAND :]).astype(jnp.bfloat16)

    def own_grads(b):
        cols = pl.ds(b * WIDTH, WIDTH)
        own_grad[:, cols] = mm(dall[OWN:BELOW, :], w[cols, :], NT)

    for b in range(QUADS):
        edge_grads(b)
    finish(3, 0)
    give_back(True)
    finish(2, 2)
    own_grads(0)
    own_grads(1)
    finish(3, 1)
    own_grads(2)
    own_grads(3)
    finish(3, 2)
    finish(2, 3)
    give_back(False)

    for b in range(QUADS):
        cols = pl.ds(b * WIDTH, WIDTH)
        value = own_grad[:, cols] + mm(unpack[...], back[:, cols])
        gi[BAND : OWN_N - BAND, cols] = value[BAND : OWN_N - BAND].astype(jnp.bfloat16)
        gi[:BAND, cols] = (value[:BAND] + lat_in[:BAND, cols].astype(jnp.float32)).astype(jnp.bfloat16)
        gi[OWN_N - BAND :, cols] = (
            value[OWN_N - BAND :] + lat_in[BAND:, cols].astype(jnp.float32)
        ).astype(jnp.bfloat16)

    finish(3, 3)


def copy_kernel(gi_in, gw_in, gi, gw):
    gi[...] = gi_in[...]
    gw[...] = gw_in[...]


def handed_over(gi, gw):
    vmem = pl.BlockSpec(memory_space=pltpu.VMEM)
    return pl.pallas_call(
        copy_kernel,
        out_shape=[jax.ShapeDtypeStruct(t.shape, t.dtype) for t in (gi, gw)],
        in_specs=[vmem] * 2,
        out_specs=[vmem] * 2,
        name="hand_over",
    )(gi, gw)


def fused(x, go, w, scale):
    bf, f32 = jnp.bfloat16, jnp.float32
    kinds = (bf, bf, bf, f32)
    pack, side, unpack, unside = packing()
    scratch = [
        pltpu.VMEM((OWN_N, D), bf),
        pltpu.VMEM((D, 3 * D), bf),
        pltpu.VMEM((SIDES, PACKED), bf),
        pltpu.VMEM((OWN_N, PACKED), bf),
        pltpu.VMEM((PACKED, SIDES), bf),
        pltpu.VMEM((TOKENS, D), bf),
        pltpu.VMEM((PACKED, D), bf),
        pltpu.VMEM((PACKED, D), bf),
        pltpu.VMEM((OWN_N, D), bf),
        pltpu.VMEM((TOKENS, D), bf),
        pltpu.VMEM((TOKENS, D), bf),
        pltpu.VMEM((TOKENS, 3 * D), bf),
        pltpu.VMEM((TOKENS, WIDTH), f32),
        pltpu.VMEM((TOKENS, WIDTH), f32),
        pltpu.VMEM((5, KEYS, WIDTH), f32),
        pltpu.VMEM((WIDTH, WIDTH), bf),
        pltpu.VMEM((D, TOKENS), bf),
        pltpu.VMEM((QUADS, 3, D, WIDTH), bf),
    ]
    scratch += [pltpu.VMEM((QUADS, 3, LEFT[s - 1], WIDTH), kinds[s]) for s in range(1, 4)]
    scratch += [pltpu.VMEM((QUADS, 3, STAGES[s] - 1, LEFT[s], WIDTH), kinds[s]) for s in range(4)]
    scratch += [
        pltpu.VMEM((PACKED, D), bf),
        pltpu.VMEM((2 * BAND, D), bf),
        pltpu.VMEM((2 * BAND, D), bf),
        pltpu.VMEM((OWN_N, D), f32),
        pltpu.VMEM((OWN + TOKENS - BELOW - ABOVE, D), f32),
        pltpu.SemaphoreType.DMA((5,)),
        pltpu.SemaphoreType.DMA((QUADS, 4, 3, 3)),
        pltpu.SemaphoreType.DMA((QUADS, 4, 3, 3)),
        pltpu.SemaphoreType.DMA((8,)),
        pltpu.SemaphoreType.DMA((8,)),
        pltpu.SemaphoreType.DMA((8,)),
        pltpu.SemaphoreType.DMA((8,)),
    ]
    vmem = pl.BlockSpec(memory_space=pltpu.VMEM)
    anywhere = pl.BlockSpec(memory_space=pl.ANY)
    return pl.pallas_call(
        functools.partial(fused_kernel, scale),
        out_shape=[
            jax.ShapeDtypeStruct((OWN_N, D), bf),
            jax.ShapeDtypeStruct((8, 3 * D), f32),
        ],
        in_specs=[vmem, vmem] + [anywhere] * 5,
        out_specs=[vmem, vmem],
        scratch_shapes=scratch,
        compiler_params=pltpu.CompilerParams(
            collective_id=0, has_side_effects=True, vmem_limit_bytes=61 * 2**20
        ),
        name="attention_backward",
    )(x, pack, go, w, side, unpack, unside)


def body(inputs, grad_out, w_qkv):
    scale = float(2 * 128 * 256) ** -0.5
    gi, gw = fused(inputs.reshape(OWN_N, D), grad_out.reshape(OWN_N, D), w_qkv, scale)
    gi, gw = handed_over(gi, gw)
    return gi.reshape(inputs.shape), gw


def solution(mesh):
    in_specs = (P("dp", "lat", "lon", None), P("dp", "lat", "lon", None), P())
    out_specs = (P("dp", "lat", "lon", None), P(("dp", "lat", "lon"), None))
    return jax.shard_map(body, mesh=mesh, in_specs=in_specs, out_specs=out_specs, check_vma=False)
```

```python
import functools

import jax
import jax.numpy as jnp
import numpy as np
from jax import lax
from jax.experimental import pallas as pl
from jax.experimental.pallas import tpu as pltpu
from jax.sharding import PartitionSpec as P

WIN = 13
MARGIN = WIN // 2
HEAD = 64
QUAD = 4
WIDTH = QUAD * HEAD
LAT_DEV = 32
LON_DEV = 16
ROW_T = 4
TILES = LAT_DEV // ROW_T
QUERIES = ROW_T * LON_DEV
KEY_ROWS = ROW_T + WIN - 1
SIDE = 2 * MARGIN
KEYS_A = KEY_ROWS * LON_DEV
KEYS_B = KEY_ROWS * SIDE
KEYS = KEYS_A + KEYS_B
PAD_ROWS = 2
OWN = (PAD_ROWS + MARGIN) * LON_DEV
OWN_N = LAT_DEV * LON_DEV
SPLIT = (PAD_ROWS + LAT_DEV + SIDE) * LON_DEV
TOKENS = 1280
D = 1024
NT = (((1,), (1,)), ((), ()))
TN = (((0,), (0,)), ((), ()))
NN = (((1,), (0,)), ((), ()))
MESH = pl.DeviceIdType.MESH


def mm(a, b, dims=NN):
    return lax.dot_general(a, b, dims, preferred_element_type=jnp.float32)


def key_tile(t, first_band, last_band):
    lead = jnp.logical_and(first_band, t == 0).astype(jnp.int32)
    tail = jnp.logical_and(last_band, t == TILES - 1).astype(jnp.int32)
    return t + lead - tail


def window_bias(t, top, keys, side, band_start, total_rows):
    kk = lax.broadcasted_iota(jnp.int32, (keys, WIDTH), 0)
    qq = lax.broadcasted_iota(jnp.int32, (keys, WIDTH), 1) & (QUERIES - 1)
    i, j = qq >> 4, qq & 15
    if side:
        r = (kk * 171) >> 11
        c = kk - r * SIDE
        col = jnp.where(c < MARGIN, c - MARGIN, c + (LON_DEV - MARGIN))
    else:
        r, col = kk >> 4, kk & 15
    first = band_start + ROW_T * t
    key_row = band_start + ROW_T * top - MARGIN + r
    start = jnp.clip(first + i - MARGIN, 0, total_rows - WIN)
    off = key_row - start
    away = col - j
    inside = (off >= 0) & (off < WIN) & (away >= -MARGIN) & (away <= MARGIN)
    return jnp.where(inside, 0.0, -1e30).astype(jnp.float32)


def spread(tile, same_head):
    return jnp.concatenate([tile] * QUAD, axis=0) * same_head


def attend(t, top, cols, q, kv, vv, go, bias, same, dk, dv, dq):
    own = pl.ds(t * QUERIES, QUERIES)
    ka = pl.ds(pl.multiple_of(PAD_ROWS * LON_DEV + top * QUERIES, 32), KEYS_A)
    kb = pl.ds(pl.multiple_of(SPLIT + top * ROW_T * SIDE, 16), KEYS_B)
    kind = min(t, 2) if t < TILES - 2 else t - TILES + 5
    same_head = same[...]
    bq = spread(q[own, cols], same_head)
    bg = spread(go[own, cols], same_head)
    keys_a, keys_b = kv[ka, cols], kv[kb, cols]
    sa = mm(keys_a, bq, NT) + bias[kind, :KEYS_A, :]
    sb = mm(keys_b, bq, NT) + bias[kind, KEYS_A:, :]
    peak = jnp.maximum(jnp.max(sa, axis=0, keepdims=True), jnp.max(sb, axis=0, keepdims=True))
    pa = jnp.exp(sa - peak)
    pb = jnp.exp(sb - peak)
    da = mm(vv[ka, cols], bg, NT)
    db = mm(vv[kb, cols], bg, NT)
    inv = 1.0 / (jnp.sum(pa, axis=0, keepdims=True) + jnp.sum(pb, axis=0, keepdims=True))
    delta = (
        jnp.sum(pa * da, axis=0, keepdims=True) + jnp.sum(pb * db, axis=0, keepdims=True)
    ) * inv
    pa = pa * inv
    pb = pb * inv
    aa = pa.astype(jnp.bfloat16)
    ab = pb.astype(jnp.bfloat16)
    ea = (pa * (da - delta)).astype(jnp.bfloat16)
    eb = (pb * (db - delta)).astype(jnp.bfloat16)
    dk[ka, :] += mm(ea, bq)
    dk[kb, :] += mm(eb, bq)
    dv[ka, :] += mm(aa, bg)
    dv[kb, :] += mm(ab, bg)
    mixed = (mm(ea, keys_a, TN) + mm(eb, keys_b, TN)) * same_head.astype(jnp.float32)
    total = mixed[:QUERIES]
    for h in range(1, QUAD):
        total = total + mixed[h * QUERIES : (h + 1) * QUERIES]
    rows = pl.ds(OWN + t * QUERIES, QUERIES)
    dq[rows, cols] = (total * HEAD**-0.5).astype(jnp.bfloat16)


STAGES = (2, 4, 4, 4)
LEFT = (512, 128, 32, 8)


def place():
    lon = lax.axis_index("lon")
    return lax.axis_index("dp"), lax.axis_index("lat"), lon >> 3, (lon >> 1) & 3, lon & 1


def device(xlo, y, xhi, z, core):
    return (xlo, y, xhi * 8 + z * 2 + core)


ORDERS = ("zyx", "yxz", "xzy")


def along(axis):
    xlo, y, xhi, z, core = place()
    me = {"x": xhi * 2 + xlo, "y": y, "z": z}[axis]
    others = []
    for step in (1, 3, 2):
        to = (me + step) & 3
        if axis == "z":
            others.append((to, device(xlo, y, xhi, to, core)))
        elif axis == "y":
            others.append((to, device(xlo, to, xhi, z, core)))
        else:
            others.append((to, device(to & 1, y, to >> 1, z, core)))
    return me, others


def peers(stage, i):
    if stage == 0:
        xlo, y, xhi, z, core = place()
        return core, [(1 - core, device(xlo, y, xhi, z, 1 - core))]
    return along(ORDERS[i][stage - 1])


def by_owner(value, order):
    blocks = []
    for core in range(2):
        for n in range(64):
            at = dict(zip(order, (n >> 4, (n >> 2) & 3, n & 3)))
            xlo, xhi = at["x"] & 1, at["x"] >> 1
            start = ((((xlo * 4 + at["y"]) * 2 + xhi) * 4 + at["z"]) * 2 + core) * 8
            blocks.append(value[start : start + 8])
    return jnp.concatenate(blocks, axis=0)


SLOTS = ((0, 192, 0, -1), (192, 192, 0, 1), (384, 48, -1, -1), (432, 48, -1, 1), (480, 48, 1, -1), (528, 48, 1, 1))
OPPOSITE = (1, 0, 5, 4, 3, 2)
PACKED = 576
SIDES = TOKENS - SPLIT
ABOVE = PAD_ROWS * LON_DEV
BELOW = OWN + OWN_N
BAND = MARGIN * LON_DEV
QUADS = D // WIDTH


def packing():
    pack = np.zeros((PACKED, OWN_N), np.float32)
    side = np.zeros((SIDES, PACKED), np.float32)
    for start, size, dy, dx in SLOTS:
        count = LAT_DEV if dy == 0 else MARGIN
        for r in range(count):
            for c in range(MARGIN):
                row = r + (LAT_DEV - MARGIN if dy > 0 else 0)
                col = c + (LON_DEV - MARGIN if dx > 0 else 0)
                pack[start + r * MARGIN + c, row * LON_DEV + col] = 1
                row = r + (MARGIN if dy == 0 else 0 if dy < 0 else LAT_DEV + MARGIN)
                col = c + (MARGIN if dx > 0 else 0)
                side[row * SIDE + col, start + r * MARGIN + c] = 1
    return [jnp.asarray(m, jnp.bfloat16) for m in (pack, side, pack.T, side.T)]


def fused_kernel(
    scale, x, pack, go_hbm, w_hbm, side_hbm, unpack_hbm, unside_hbm, gi, gw,
    go, w, side, unpack, unside, xe, packed, halo, q, k, v, dall, dk, dv, bias, same, xt,
    part, held1, held2, held3, got0, got1, got2, got3,
    back, lat_out, lat_in, own_grad,
    load, send, recv, halo_send, halo_recv, back_send, back_recv,
):
    dp, lat, lon = lax.axis_index("dp"), lax.axis_index("lat"), lax.axis_index("lon")
    lats, lons = lax.axis_size("lat"), lax.axis_size("lon")
    band_start = lat * LAT_DEV
    total_rows = LAT_DEV * lats
    first_band, last_band = lat == 0, lat == lats - 1
    held = (part, held1, held2, held3)
    got = (got0, got1, got2, got3)

    loads = [
        pltpu.make_async_copy(w_hbm, w, load.at[0]),
        pltpu.make_async_copy(go_hbm, go, load.at[1]),
        pltpu.make_async_copy(side_hbm, side, load.at[2]),
        pltpu.make_async_copy(unpack_hbm, unpack, load.at[3]),
        pltpu.make_async_copy(unside_hbm, unside, load.at[4]),
    ]
    for copy in loads:
        copy.start()

    def when_there(dy, act):
        if dy == 0:
            act()
        else:
            pl.when(lat > 0 if dy < 0 else lat < lats - 1)(act)

    def neighbour(dy, dx):
        return (dp, lat + dy, lax.rem(lon + dx + lons, lons))

    moves = [(dy, dx) for _, _, dy, dx in SLOTS] + [(-1, 0), (1, 0)]

    packed[...] = mm(pack[...], x[...]).astype(jnp.bfloat16)

    barrier = pltpu.get_barrier_semaphore()
    count = 0
    for others in (peers(0, 0)[1], along("x")[1], along("y")[1], along("z")[1]):
        for _, dev in others:
            pl.semaphore_signal(barrier, inc=1, device_id=dev, device_id_type=MESH)
            count += 1
    for dy, dx in moves:
        @functools.partial(when_there, dy)
        def _():
            pl.semaphore_signal(barrier, inc=1, device_id=neighbour(dy, dx), device_id_type=MESH)
    count = count + 2 + 3 * (lat > 0).astype(jnp.int32) + 3 * (lat < lats - 1).astype(jnp.int32)
    pl.semaphore_wait(barrier, count)

    def exchange(source, target, up, down, into_up, into_down, sends, recvs, sending):
        for n, (dy, dx) in enumerate(moves):
            @functools.partial(when_there, dy)
            def _():
                if n < 6:
                    other = OPPOSITE[n]
                    start, size = SLOTS[n][:2]
                    there = SLOTS[other][0]
                    src = source.at[pl.ds(start, size), :]
                    far, near = target.at[pl.ds(there, size), :], target.at[pl.ds(start, size), :]
                else:
                    other = 13 - n
                    src = (up, down)[n - 6]
                    far, near = (into_down, into_up) if n == 6 else (into_up, into_down)
                copy = pltpu.make_async_remote_copy(
                    src_ref=src,
                    dst_ref=far if sending else near,
                    send_sem=sends.at[n],
                    recv_sem=recvs.at[other if sending else n],
                    device_id=neighbour(dy, dx),
                    device_id_type=MESH,
                )
                if sending:
                    copy.start()
                else:
                    copy.wait()

    def halo_exchange(sending):
        exchange(
            packed, halo, x.at[pl.ds(0, BAND), :], x.at[pl.ds(OWN_N - BAND, BAND), :],
            xe.at[pl.ds(ABOVE, BAND), :], xe.at[pl.ds(BELOW, BAND), :],
            halo_send, halo_recv, sending,
        )

    def give_back(sending):
        exchange(
            packed, back, lat_out.at[pl.ds(0, BAND), :], lat_out.at[pl.ds(BAND, BAND), :],
            lat_in.at[pl.ds(0, BAND), :], lat_in.at[pl.ds(BAND, BAND), :],
            back_send, back_recv, sending,
        )

    halo_exchange(True)

    for there, slot in ((lat > 0, 384), (lat < lats - 1, 480)):
        @pl.when(jnp.logical_not(there))
        def _():
            zero = jnp.zeros((96, D), jnp.bfloat16)
            halo[slot : slot + 96, :] = zero
            back[slot : slot + 96, :] = zero
            at = ABOVE if slot == 384 else BELOW
            xe[at : at + BAND, :] = zero
            at = 0 if slot == 384 else BAND
            lat_in[at : at + BAND, :] = zero

    xe[:ABOVE, :] = jnp.zeros((ABOVE, D), jnp.bfloat16)
    xe[OWN : OWN + OWN_N, :] = x[...]
    row = lax.broadcasted_iota(jnp.int32, (WIDTH, WIDTH), 0)
    col = lax.broadcasted_iota(jnp.int32, (WIDTH, WIDTH), 1)
    same[...] = jnp.where((row >> 6) == (col >> 6), 1.0, 0.0).astype(jnp.bfloat16)

    loads[0].wait()

    @pl.loop(0, QUADS)
    def _(b):
        cols = pl.ds(pl.multiple_of(b * WIDTH, WIDTH), WIDTH)
        kcols = pl.ds(pl.multiple_of(D + b * WIDTH, WIDTH), WIDTH)
        vcols = pl.ds(pl.multiple_of(2 * D + b * WIDTH, WIDTH), WIDTH)
        q[:, cols] = mm(x[...], w[:, cols]).astype(jnp.bfloat16) * jnp.bfloat16(0.125)
        k[OWN : OWN + OWN_N, cols] = mm(x[...], w[:, kcols]).astype(jnp.bfloat16)
        v[OWN : OWN + OWN_N, cols] = mm(x[...], w[:, vcols]).astype(jnp.bfloat16)

    @pl.loop(0, 5)
    def _(n):
        t = n + (TILES - 5) * (n >= 3).astype(jnp.int32)
        top = key_tile(t, first_band, last_band)
        bias[n, :KEYS_A, :] = window_bias(t, top, KEYS_A, False, band_start, total_rows)
        bias[n, KEYS_A:, :] = window_bias(t, top, KEYS_B, True, band_start, total_rows)

    for copy in loads[1:]:
        copy.wait()
    halo_exchange(False)
    xe[SPLIT:, :] = mm(side[...], halo[...]).astype(jnp.bfloat16)

    @pl.loop(0, QUADS)
    def _(b):
        cols = pl.ds(pl.multiple_of(b * WIDTH, WIDTH), WIDTH)
        kcols = pl.ds(pl.multiple_of(D + b * WIDTH, WIDTH), WIDTH)
        vcols = pl.ds(pl.multiple_of(2 * D + b * WIDTH, WIDTH), WIDTH)
        outer = jnp.concatenate([xe[:OWN, :], xe[BELOW:, :]], axis=0)
        for into, wcols in ((k, kcols), (v, vcols)):
            value = mm(outer, w[:, wcols]).astype(jnp.bfloat16)
            into[:OWN, cols] = value[:OWN]
            into[BELOW:, cols] = value[OWN:]
        rows = pl.ds(pl.multiple_of(b * 256, 256), 256)
        xt[rows, :] = xe[:, rows].T

    def copies(c, stage, i):
        return [
            pltpu.make_async_remote_copy(
                src_ref=held[stage].at[c, i, pl.ds(to * LEFT[stage], LEFT[stage]), :],
                dst_ref=got[stage].at[c, i, n],
                send_sem=send.at[c, stage, i, n],
                recv_sem=recv.at[c, stage, i, n],
                device_id=dev,
                device_id_type=MESH,
            )
            for n, (to, dev) in enumerate(peers(stage, i)[1])
        ]

    def begin(c, stage, i):
        for copy in copies(c, stage, i):
            copy.start()

    def finish(c, stage):
        for i in (1, 2, 0):
            for copy in copies(c, stage, i):
                copy.wait()
            me, others = peers(stage, i)
            rows = pl.ds(pl.multiple_of(me * LEFT[stage], LEFT[stage]), LEFT[stage])
            value = held[stage][c, i, rows, :].astype(jnp.float32)
            for n in range(len(others)):
                value = value + got[stage][c, i, n].astype(jnp.float32)
            if stage == 3:
                at = i * D + c * WIDTH
                at = at if isinstance(at, int) else pl.multiple_of(at, WIDTH)
                gw[:, pl.ds(at, WIDTH)] = value
            else:
                held[stage + 1][c, i] = value.astype(held[stage + 1].dtype)
                begin(c, stage + 1, i)

    @pl.loop(0, QUADS)
    def _(g):
        cols = pl.ds(pl.multiple_of(g * WIDTH, WIDTH), WIDTH)
        kcols = pl.ds(pl.multiple_of(D + g * WIDTH, WIDTH), WIDTH)
        vcols = pl.ds(pl.multiple_of(2 * D + g * WIDTH, WIDTH), WIDTH)
        dk[...] = jnp.zeros_like(dk)
        dv[...] = jnp.zeros_like(dv)

        def tiles(a, b):
            for t in range(a, b):
                top = key_tile(t, first_band, last_band)
                attend(t, top, cols, q, k, v, go, bias, same, dk, dv, dall)

        tiles(0, 5)

        @pl.when(g >= 1)
        def _():
            finish(g - 1, 0)

        tiles(5, TILES)

        @pl.when(g >= 2)
        def _():
            finish(g - 2, 2)

        dall[:, kcols] = dk[...].astype(jnp.bfloat16)
        dall[:, vcols] = dv[...].astype(jnp.bfloat16)
        mine = pl.ds(OWN, OWN_N)
        for i, tokens, wide in ((1, slice(None), kcols), (2, slice(None), vcols), (0, mine, cols)):
            value = mm(xt[:, tokens], dall[tokens, wide]) * scale
            part[g, i] = by_owner(value, ORDERS[i]).astype(jnp.bfloat16)
            begin(g, 0, i)

        @pl.when(g >= 1)
        def _():
            finish(g - 1, 1)

        @pl.when(g >= 2)
        def _():
            finish(g - 2, 3)

    def edge_grads(b):
        cols = pl.ds(b * WIDTH, WIDTH)
        rows = jnp.concatenate([dall[ABOVE:OWN, D:], dall[BELOW:, D:]], axis=0)
        value = mm(rows, w[cols, D:], NT).astype(jnp.bfloat16)
        lat_out[:, cols] = value[: 2 * BAND]
        packed[:, cols] = mm(unside[...], value[2 * BAND :]).astype(jnp.bfloat16)

    def own_grads(b):
        cols = pl.ds(b * WIDTH, WIDTH)
        own_grad[:, cols] = mm(dall[OWN:BELOW, :], w[cols, :], NT)

    edge_grads(0)
    edge_grads(1)
    finish(3, 0)
    finish(2, 2)
    edge_grads(2)
    edge_grads(3)
    give_back(True)
    finish(3, 1)
    own_grads(0)
    own_grads(1)
    finish(3, 2)
    own_grads(2)
    own_grads(3)
    finish(2, 3)
    give_back(False)

    for b in range(QUADS):
        cols = pl.ds(b * WIDTH, WIDTH)
        value = own_grad[:, cols] + mm(unpack[...], back[:, cols])
        gi[BAND : OWN_N - BAND, cols] = value[BAND : OWN_N - BAND].astype(jnp.bfloat16)
        gi[:BAND, cols] = (value[:BAND] + lat_in[:BAND, cols].astype(jnp.float32)).astype(jnp.bfloat16)
        gi[OWN_N - BAND :, cols] = (
            value[OWN_N - BAND :] + lat_in[BAND:, cols].astype(jnp.float32)
        ).astype(jnp.bfloat16)

    finish(3, 3)


def copy_kernel(gi_in, gw_in, gi, gw):
    gi[...] = gi_in[...]
    gw[...] = gw_in[...]


def handed_over(gi, gw):
    vmem = pl.BlockSpec(memory_space=pltpu.VMEM)
    return pl.pallas_call(
        copy_kernel,
        out_shape=[jax.ShapeDtypeStruct(t.shape, t.dtype) for t in (gi, gw)],
        in_specs=[vmem] * 2,
        out_specs=[vmem] * 2,
        name="hand_over",
    )(gi, gw)


def fused(x, go, w, scale):
    bf, f32 = jnp.bfloat16, jnp.float32
    kinds = (bf, bf, bf, f32)
    pack, side, unpack, unside = packing()
    scratch = [
        pltpu.VMEM((OWN_N, D), bf),
        pltpu.VMEM((D, 3 * D), bf),
        pltpu.VMEM((SIDES, PACKED), bf),
        pltpu.VMEM((OWN_N, PACKED), bf),
        pltpu.VMEM((PACKED, SIDES), bf),
        pltpu.VMEM((TOKENS, D), bf),
        pltpu.VMEM((PACKED, D), bf),
        pltpu.VMEM((PACKED, D), bf),
        pltpu.VMEM((OWN_N, D), bf),
        pltpu.VMEM((TOKENS, D), bf),
        pltpu.VMEM((TOKENS, D), bf),
        pltpu.VMEM((TOKENS, 3 * D), bf),
        pltpu.VMEM((TOKENS, WIDTH), f32),
        pltpu.VMEM((TOKENS, WIDTH), f32),
        pltpu.VMEM((5, KEYS, WIDTH), f32),
        pltpu.VMEM((WIDTH, WIDTH), bf),
        pltpu.VMEM((D, TOKENS), bf),
        pltpu.VMEM((QUADS, 3, D, WIDTH), bf),
    ]
    scratch += [pltpu.VMEM((QUADS, 3, LEFT[s - 1], WIDTH), kinds[s]) for s in range(1, 4)]
    scratch += [pltpu.VMEM((QUADS, 3, STAGES[s] - 1, LEFT[s], WIDTH), kinds[s]) for s in range(4)]
    scratch += [
        pltpu.VMEM((PACKED, D), bf),
        pltpu.VMEM((2 * BAND, D), bf),
        pltpu.VMEM((2 * BAND, D), bf),
        pltpu.VMEM((OWN_N, D), f32),
        pltpu.SemaphoreType.DMA((5,)),
        pltpu.SemaphoreType.DMA((QUADS, 4, 3, 3)),
        pltpu.SemaphoreType.DMA((QUADS, 4, 3, 3)),
        pltpu.SemaphoreType.DMA((8,)),
        pltpu.SemaphoreType.DMA((8,)),
        pltpu.SemaphoreType.DMA((8,)),
        pltpu.SemaphoreType.DMA((8,)),
    ]
    vmem = pl.BlockSpec(memory_space=pltpu.VMEM)
    anywhere = pl.BlockSpec(memory_space=pl.ANY)
    return pl.pallas_call(
        functools.partial(fused_kernel, scale),
        out_shape=[
            jax.ShapeDtypeStruct((OWN_N, D), bf),
            jax.ShapeDtypeStruct((8, 3 * D), f32),
        ],
        in_specs=[vmem, vmem] + [anywhere] * 5,
        out_specs=[vmem, vmem],
        scratch_shapes=scratch,
        compiler_params=pltpu.CompilerParams(
            collective_id=0, has_side_effects=True, vmem_limit_bytes=61 * 2**20
        ),
        name="attention_backward",
    )(x, pack, go, w, side, unpack, unside)


def body(inputs, grad_out, w_qkv):
    scale = float(2 * 128 * 256) ** -0.5
    gi, gw = fused(inputs.reshape(OWN_N, D), grad_out.reshape(OWN_N, D), w_qkv, scale)
    gi, gw = handed_over(gi, gw)
    return gi.reshape(inputs.shape), gw


def solution(mesh):
    in_specs = (P("dp", "lat", "lon", None), P("dp", "lat", "lon", None), P())
    out_specs = (P("dp", "lat", "lon", None), P(("dp", "lat", "lon"), None))
    return jax.shard_map(body, mesh=mesh, in_specs=in_specs, out_specs=out_specs, check_vma=False)
```
